256 devices in a mesh: tile: 64 (over x_lo, y, z), mode: 4 (over x_hi, core).
Axes of the slice: x: 4 (x_hi: 2, x_lo: 2; x = x_hi * 2 + x_lo), y: 4, z: 8, core: 2. Of those that a mesh axis runs over, the one named last changes fastest.
Arguments:
- object_field: float32 [2, 512, 32768], P(None, 'mode', 'tile'), may hold values from -5 to 5
- probe: float32 [8, 2, 256, 256], P('mode'), may hold values from -1.5 to 1.5
- measured: float32 [768, 256, 256], P(('tile', 'mode')), may hold values from 0.3 to 3
- scan_rows: int32 [768], P(('tile', 'mode')), may hold values from 0 to 256
- scan_cols: int32 [768], P(('tile', 'mode')), may hold values from 0 to 512
- counts: int32 [64], P('tile'), may hold values from 1 to 12, 240 in all
Outputs:
- object_out: float32 [2, 512, 32768], P(None, 'mode', 'tile')
- probe_out: float32 [8, 2, 256, 256], P('mode', None, 'tile')
The draws below stay inside these ranges and needn't reach their ends.
Inputs may be any that keep to these rules, and one draw needn't show every extreme that they name: Slot j of tile t holds a scan exactly when j < counts[t]; some tile has all 12 slots live.
All inputs are finite; a program needn't handle non-finite values. No bound on the sum of `counts` on one device may be relied on, other than what follows from the above.
Results may differ from the reference program's by a relative error of at most 0.0014.
Values may be sent and summed in bfloat16 or wider, within the bound.
A program may use at most 128 MiB of HBM per device.

```python
import math
import jax
import jax.numpy as jnp
import numpy as np
from jax import lax

P_SIZE = 256
MODES = 8
OR = 512
TW = 512
CAP = 12
SCANS = 240
OC = 32768
SLOTS = 768
N_TILE = 64


def place_ends(values, stream_key, least, largest):
    dims = values.shape
    index_at = [jax.random.randint(jax.random.fold_in(stream_key, axis), (), 0, dims[axis]) for axis in range(len(dims))]
    values = values.at[tuple(index_at)].set(least)
    longest = dims.index(max(dims))
    index_at[longest] = (index_at[longest] + 1) % dims[longest]
    return values.at[tuple(index_at)].set(largest)


def block_scale(rng, extent, cuts, low, largest):
    level = 1.0
    for dim, parts in cuts:
        steps = jax.random.uniform(jax.random.fold_in(jax.random.fold_in(rng, 6), dim), (parts,), jnp.float32, low / len(cuts), largest / len(cuts))
        level = level * jnp.repeat(jnp.exp(steps), extent[dim] // parts).reshape((-1,) + (1,) * (len(extent) - 1 - dim))
    return level


def profile(number_of, total, limit, skew):
    weights = [(1 << 20) // math.isqrt(standing ** skew) + 1 for standing in range(2, number_of + 1)]
    surplus, given = total - limit - (number_of - 1), [1] * (number_of - 1)
    while surplus > 0:
        free = [i for i in range(number_of - 1) if given[i] < limit]
        whole, remaining = sum([weights[i] for i in free]), surplus
        for i in free:
            extra = min(limit - given[i], max(1, remaining * weights[i] // whole), surplus)
            given[i] = given[i] + extra
            surplus = surplus - extra
    return np.array([limit] + given)


def uneven_parts(rng, count, total, limit, lean):
    if count == 2:
        one = jax.random.randint(rng, (), max(1, total - limit), min(limit, total - 1) + 1)
        return jnp.stack([one, total - one])
    tallies = jnp.asarray(profile(count, total, limit, lean), jnp.int32)
    couples = (count - 1) // 2
    source_of, taker = tallies[1:1 + 2 * couples:2], tallies[2:2 + 2 * couples:2]
    room = jnp.minimum(source_of - 1, limit - taker)
    shifted = jax.random.randint(jax.random.fold_in(rng, 1), (couples,), 0, 1 << 20) % (room + 1)
    tallies = tallies.at[1:1 + 2 * couples:2].set(source_of - shifted).at[2:2 + 2 * couples:2].set(taker + shifted)
    return tallies[jax.random.permutation(jax.random.fold_in(rng, 2), count)]


def bell_draw(stream_key, shape, scale, bound, shards=(), held_as=jnp.bfloat16):
    array = scale * jax.random.normal(stream_key, shape, jnp.float32)
    if shards:
        array = array * block_scale(stream_key, shape, shards, -0.22, 0.18)
    return jnp.clip(array, -bound, bound).astype(held_as)


def setup_inputs(seed: int = 0) -> dict:
    arg_keys = jax.random.split(jax.random.key(seed), 7)
    object_field = bell_draw(arg_keys[0], (2, OR, OC), 0.7, 5.0, ((1, 4), (2, 64)), jnp.float32)
    probe = bell_draw(arg_keys[1], (MODES, 2, P_SIZE, P_SIZE), 0.25, 1.5, ((0, 4),), jnp.float32)
    measured = jnp.clip(jnp.exp(math.log(3.0) - 2.3025851 * jax.random.uniform(arg_keys[2], (SLOTS, P_SIZE, P_SIZE), jnp.float32) ** block_scale(arg_keys[2], (SLOTS, P_SIZE, P_SIZE), ((0, 256),), -0.2, 0.2)), 0.3, 3.0)
    scan_rows = place_ends(jax.random.randint(arg_keys[3], (SLOTS,), 0, OR - P_SIZE + 1), jax.random.fold_in(arg_keys[3], 1), 0, OR - P_SIZE).astype(jnp.int32)
    scan_cols = place_ends(jax.random.randint(arg_keys[4], (SLOTS,), 0, TW + 1), jax.random.fold_in(arg_keys[4], 1), 0, TW).astype(jnp.int32)
    counts = uneven_parts(arg_keys[5], N_TILE, SCANS, CAP, 2).astype(jnp.int32)
    return {"object_field": object_field, "probe": probe, "measured": measured, "scan_rows": scan_rows, "scan_cols": scan_cols, "counts": counts}


object_reg = 0.5
probe_reg = 1.0
power_floor = 0.25

def dft_blocks(length):
    positions = jnp.arange(length, dtype=jnp.int32)
    product = positions[:, None] * positions[None, :] % length
    angles = product.astype(jnp.float32) * (2.0 * jnp.pi / length)
    scaling = 1.0 / jnp.sqrt(jnp.float32(length))
    real_part = (jnp.cos(angles) * scaling).astype(jnp.bfloat16)
    imag_part = (-jnp.sin(angles) * scaling).astype(jnp.bfloat16)
    forward = jnp.concatenate([jnp.concatenate([real_part, imag_part], 1), jnp.concatenate([-imag_part, real_part], 1)], 0)
    inverse = jnp.concatenate([jnp.concatenate([real_part, -imag_part], 1), jnp.concatenate([imag_part, real_part], 1)], 0)
    return (forward, inverse)

def along_last(values, matrix):
    flattened = values.reshape(values.shape[0] * values.shape[1], values.shape[2])
    result = jnp.dot(flattened, matrix, preferred_element_type=jnp.float32)
    return result.reshape(values.shape[0], values.shape[1], matrix.shape[1])

def swap_axes(values):
    batch_count, length, doubled = values.shape
    half_width = doubled // 2
    return values.reshape(batch_count, length, 2, half_width).transpose(0, 3, 2, 1).reshape(batch_count, half_width, 2 * length)

def correction(object_patch, probe_half, amplitude, forward, inverse):
    length = amplitude.shape[0]
    patch_re = object_patch[0].astype(jnp.float32)
    patch_im = object_patch[1].astype(jnp.float32)
    probe_re = probe_half[:, 0].astype(jnp.float32)
    probe_im = probe_half[:, 1].astype(jnp.float32)
    wave = jnp.concatenate([probe_re * patch_re - probe_im * patch_im, probe_re * patch_im + probe_im * patch_re], 2).astype(jnp.bfloat16)
    half_spectrum = along_last(wave, forward).astype(jnp.bfloat16)
    spectrum = along_last(swap_axes(half_spectrum), forward)
    spec_re = spectrum[:, :, :length]
    spec_im = spectrum[:, :, length:]
    power_sum = lax.optimization_barrier(jnp.sum(spec_re * spec_re + spec_im * spec_im, 0))
    factor = amplitude.T / jnp.sqrt(jnp.maximum(power_sum, power_floor)) - 1.0
    difference = (spectrum * jnp.concatenate([factor, factor], 1)[None]).astype(jnp.bfloat16)
    back_half = along_last(difference, inverse).astype(jnp.bfloat16)
    back = along_last(swap_axes(back_half), inverse)
    return (back[:, :, :length], back[:, :, length:])

def reference(object_field, probe, measured, scan_rows, scan_cols, counts):
    forward, inverse = dft_blocks(P_SIZE)
    margin = P_SIZE // 2
    object_half = object_field.astype(jnp.bfloat16)
    probe_half = probe.astype(jnp.bfloat16)
    padded = jnp.pad(object_half, ((0, 0), (0, 0), (margin, margin)))
    probe_re = probe_half[:, 0].astype(jnp.float32)
    probe_im = probe_half[:, 1].astype(jnp.float32)
    lighting = lax.optimization_barrier(jnp.sum(probe_re * probe_re + probe_im * probe_im, 0))
    zero_index = jnp.int32(0)

    def tile_step(tile_index, state_now):

        def scan_step(slot_index, accumulated):
            gradient, probe_grad, weight_sum = accumulated
            slot_global = (tile_index * CAP + slot_index).astype(jnp.int32)
            row_start = scan_rows[slot_global].astype(jnp.int32)
            col_start = (tile_index * TW + scan_cols[slot_global]).astype(jnp.int32)
            object_patch = lax.dynamic_slice(padded, (zero_index, row_start, col_start), (2, P_SIZE, P_SIZE))
            back_re, back_im = correction(object_patch, probe_half, measured[slot_global], forward, inverse)
            grad_re = lax.optimization_barrier(jnp.sum(probe_re * back_re + probe_im * back_im, 0))
            grad_im = lax.optimization_barrier(jnp.sum(probe_re * back_im - probe_im * back_re, 0))
            term = jnp.stack([grad_re, grad_im, lighting])
            previous = lax.dynamic_slice(gradient, (zero_index, row_start, col_start), (3, P_SIZE, P_SIZE))
            gradient = lax.dynamic_update_slice(gradient, previous + term, (zero_index, row_start, col_start))
            patch_re = object_patch[0].astype(jnp.float32)
            patch_im = object_patch[1].astype(jnp.float32)
            term_re = patch_re * back_re + patch_im * back_im
            term_im = patch_re * back_im - patch_im * back_re
            probe_grad = probe_grad + jnp.stack([term_re, term_im], 1)
            weight_sum = weight_sum + patch_re * patch_re + patch_im * patch_im
            return (gradient, probe_grad, weight_sum)
        return lax.fori_loop(jnp.int32(0), counts[tile_index].astype(jnp.int32), scan_step, state_now)
    initial = (jnp.zeros((3, OR, OC + P_SIZE), jnp.float32), jnp.zeros((MODES, 2, P_SIZE, P_SIZE), jnp.float32), jnp.zeros((P_SIZE, P_SIZE), jnp.float32))
    gradient, probe_grad, weight_sum = lax.fori_loop(jnp.int32(0), jnp.int32(N_TILE), tile_step, initial)
    gradient = gradient[:, :, margin:margin + OC]
    object_out = object_field + gradient[:2] / (gradient[2] + object_reg)
    probe_out = probe + probe_grad / (weight_sum + probe_reg)
    return (object_out, probe_out)
```

```python
import functools

import jax
import jax.numpy as jnp
import ml_dtypes
import numpy as np
from jax import lax
from jax.experimental import pallas as pl
from jax.experimental.pallas import tpu as pltpu
from jax.sharding import PartitionSpec as P

object_reg = 0.5
probe_reg = 1.0
N = 256
bf = jnp.bfloat16
f32 = jnp.float32

def tables():
    pos = np.arange(N)
    ang = (pos[:, None] * pos[None, :] % N) * (2.0 * np.pi / N)
    sc = 1.0 / np.sqrt(float(N))
    re = (np.cos(ang) * sc).astype(ml_dtypes.bfloat16)
    im = (-np.sin(ang) * sc).astype(ml_dtypes.bfloat16)
    forward = np.block([[re, im], [-im, re]]).astype(ml_dtypes.bfloat16)
    inverse = np.block([[re, -im], [im, re]]).astype(ml_dtypes.bfloat16)
    return forward, inverse

def dot(a, b):
    return jnp.dot(a, b, preferred_element_type=f32)

def k2_kernel(rows, cols, live, ext, probe, meas, fwd, inv, grad, pg, pw,
              ext32, patch, spec, gacc, light, UN=1):
    for c in range(2):
        ext32[c, :512, :768] = ext[c].astype(f32)
        ext32[c, :512, 768:] = jnp.zeros((512, 128), f32)
        ext32[c, 512:, :] = jnp.zeros((8, 896), f32)
    gacc[...] = jnp.zeros_like(gacc)
    pg[...] = jnp.zeros_like(pg)
    pw[...] = jnp.zeros_like(pw)
    light[...] = jnp.zeros_like(light)
    def lstep(m, _):
        re = probe[m, 0].astype(f32)
        im = probe[m, 1].astype(f32)
        light[...] += re * re + im * im
        return 0
    lax.fori_loop(0, 8, lstep, 0)

    def slot(s, _):
        @pl.when(live[s] > 0)
        def _():
            row = rows[s]
            col = cols[s]
            cb = pl.multiple_of((col // 128) * 128, 128)
            cr = col - cb
            back_shift = lax.rem(384 - cr, 384)
            rb = pl.multiple_of((row // 8) * 8, 8)
            rr = row - rb
            up = lax.rem(264 - rr, 264)
            for c in range(2):
                win = ext32[c, pl.ds(rb, 264), pl.ds(cb, 384)]
                win = pltpu.roll(win, back_shift, 1)[:, :N]
                patch[c] = pltpu.roll(win, up, 0)[:N]
            pw[...] += patch[0] * patch[0] + patch[1] * patch[1]

            def first(m, power):
                pr = probe[m, 0].astype(f32)
                pi = probe[m, 1].astype(f32)
                ar = patch[0]
                ai = patch[1]
                wave = jnp.concatenate([pr * ar - pi * ai, pr * ai + pi * ar], 1).astype(bf)
                half = dot(wave, fwd[...]).astype(bf)
                stacked = jnp.concatenate([half[:, :N], half[:, N:]], 0)
                sp = dot(inv[...], stacked)
                spec[m] = sp
                return power + sp[:N] * sp[:N] + sp[N:] * sp[N:]
            power = lax.fori_loop(0, 8, first, jnp.zeros((N, N), f32), unroll=UN)
            factor = meas[s] * lax.rsqrt(jnp.maximum(power, 0.25)) - 1.0
            patch[2] = factor

            def second(m, carry):
                gr, gi = carry
                fac = patch[2]
                sp = spec[m]
                diff = jnp.concatenate([sp[:N] * fac, sp[N:] * fac], 0).astype(bf)
                bh = dot(fwd[...], diff).astype(bf)
                wide = jnp.concatenate([bh[:N], bh[N:]], 1)
                back = dot(wide, inv[...])
                br = back[:, :N]
                bi = back[:, N:]
                pr = probe[m, 0].astype(f32)
                pi = probe[m, 1].astype(f32)
                ar = patch[0]
                ai = patch[1]
                pg[m, 0] += ar * br + ai * bi
                pg[m, 1] += ar * bi - ai * br
                return gr + pr * br + pi * bi, gi + pr * bi - pi * br
            z = jnp.zeros((N, N), f32)
            gr, gi = lax.fori_loop(0, 8, second, (z, z), unroll=UN)
            pad = jnp.zeros((N, 128), f32)
            low = jnp.zeros((8, 384), f32)
            for c, term in enumerate((gr, gi, light[...])):
                moved = pltpu.roll(jnp.concatenate([term, pad], 1), cr, 1)
                moved = pltpu.roll(jnp.concatenate([moved, low], 0), rr, 0)
                gacc[c, pl.ds(rb, 264), pl.ds(cb, 384)] += moved
        return 0
    lax.fori_loop(0, 3, slot, 0)
    grad[...] = gacc[:, :512, :768]

def k2(rows, cols, live, ext, probe, meas, UN=1):
    fwd, inv = tables()
    V = pl.BlockSpec(memory_space=pltpu.VMEM)
    S = pl.BlockSpec(memory_space=pltpu.SMEM)
    return pl.pallas_call(
        functools.partial(k2_kernel, UN=UN),
        out_shape=(jax.ShapeDtypeStruct((3, 512, 768), f32),
                   jax.ShapeDtypeStruct((8, 2, N, N), f32),
                   jax.ShapeDtypeStruct((N, N), f32)),
        in_specs=[S, S, S, V, V, V, V, V],
        out_specs=(V, V, V),
        scratch_shapes=[pltpu.VMEM((2, 520, 896), f32), pltpu.VMEM((3, N, N), f32),
                        pltpu.VMEM((8, 512, N), f32), pltpu.VMEM((3, 520, 896), f32), pltpu.VMEM((N, N), f32)],
        compiler_params=pltpu.CompilerParams(vmem_limit_bytes=60 * 2**20),
        name="refine",
    )(rows, cols, live, ext, probe, meas, jnp.asarray(fwd), jnp.asarray(inv))


def extended_2(array, sides, width):
    for axis, dim in sides:
        peers, length = (lax.axis_size(axis), array.shape[dim])
        up = [(i, (i + 1) % peers) for i in range(peers - 1)]
        down = [(j, i) for i, j in up]
        last = lax.slice_in_dim(array, length - width, length, axis=dim)
        leading = lax.slice_in_dim(array, 0, width, axis=dim)
        before = lax.ppermute(last, axis, up)
        after = lax.ppermute(leading, axis, down)
        array = jnp.concatenate([before, array, after], axis=dim)
    return array


def passed_along(block, axis, distance):
    devices = range(lax.axis_size(axis))
    route = [(i - distance, i) for i in devices if i - distance in devices]
    return lax.ppermute(block, axis, route)


def local(object_field, probe, measured, scan_rows, scan_cols, counts):
    modes_here = probe.shape[0]
    length = probe.shape[2]
    margin = length // 2
    tile_width = object_field.shape[2]
    groups = lax.axis_size("mode")
    tiles = lax.axis_size("tile")
    slots = scan_rows.shape[0]
    probe_half = probe.astype(jnp.bfloat16)
    object_half = object_field.astype(jnp.bfloat16)
    probe_all, object_rows = (
        lax.all_gather(probe_half, "mode", axis=0, tiled=True),
        lax.all_gather(object_half, "mode", axis=1, tiled=True),
    )
    extended = extended_2(object_rows, (("tile", 2),), margin)
    first_slot = lax.axis_index("mode") * slots
    live = (first_slot + jnp.arange(slots, dtype=jnp.int32) < counts[0]).astype(jnp.int32)
    gradient, probe_grad, weight_sum = k2(
        scan_rows, scan_cols, live, extended, probe_all, measured, UN=2
    )
    left_rim = gradient[:, :, :margin]
    right_rim = gradient[:, :, tile_width + margin :]
    central = gradient[:, :, margin : tile_width + margin]
    from_right = passed_along(left_rim, "tile", -1)
    from_left = passed_along(right_rim.astype(jnp.bfloat16), "tile", 1).astype(right_rim.dtype)
    central = central.at[:, :, tile_width - margin :].add(from_right)
    central = central.at[:, :, :margin].add(from_left)
    summed = lax.psum_scatter(central, "mode", scatter_dimension=1, tiled=True)
    object_out = object_field + summed[:2] / (summed[2] + object_reg)
    grouped = probe_grad.reshape(groups, 2 * modes_here, length, length)
    power_plane = weight_sum.reshape(1, 1, length, length)
    by_mode = lax.psum_scatter(grouped, "mode", scatter_dimension=0, tiled=True)
    owned = lax.psum_scatter(by_mode, "tile", scatter_dimension=2, tiled=True)
    power_band = lax.psum_scatter(power_plane, "tile", scatter_dimension=2, tiled=True)
    power_total = lax.psum(power_band, "mode")
    band_rows = length // tiles
    first_row = lax.axis_index("tile") * band_rows
    probe_rows = lax.dynamic_slice_in_dim(probe, first_row, band_rows, 2)
    steps_term = owned[0].reshape(modes_here, 2, band_rows, length)
    probe_out = probe_rows + steps_term / (power_total[0, 0] + probe_reg)
    return (object_out, probe_out)


def solution(mesh):
    return jax.shard_map(
        local,
        mesh=mesh,
        in_specs=(
            P(None, "mode", "tile"),
            P("mode", None, None, None),
            P(("tile", "mode"), None, None),
            P(("tile", "mode")),
            P(("tile", "mode")),
            P("tile"),
        ),
        out_specs=(P(None, "mode", "tile"), P("mode", None, "tile", None)),
        check_vma=False,
    )
```

```python
import functools

import jax
import jax.numpy as jnp
import ml_dtypes
import numpy as np
from jax import lax
from jax.experimental import pallas as pl
from jax.experimental.pallas import tpu as pltpu
from jax.sharding import PartitionSpec as P

object_reg = 0.5
probe_reg = 1.0
N = 256
X, Y, Z = 4, 4, 8
bf = jnp.bfloat16
f32 = jnp.float32
MESH = pl.DeviceIdType.MESH
XY = [(i, j) for i in range(X) for j in range(Y) if i or j]


def tables():
    pos = np.arange(N)
    ang = (pos[:, None] * pos[None, :] % N) * (2.0 * np.pi / N)
    sc = 1.0 / np.sqrt(float(N))
    re = (np.cos(ang) * sc).astype(ml_dtypes.bfloat16)
    im = (-np.sin(ang) * sc).astype(ml_dtypes.bfloat16)
    forward = np.block([[re, im], [-im, re]]).astype(ml_dtypes.bfloat16)
    inverse = np.block([[re, -im], [im, re]]).astype(ml_dtypes.bfloat16)
    return forward, inverse


def dot(a, b):
    return jnp.dot(a, b, preferred_element_type=f32)


def here():
    tile = lax.axis_index("tile")
    group = lax.axis_index("mode")
    x = (group // 2) * 2 + tile // (Y * Z)
    return tile, group, x, (tile // Z) % Y, tile % Z, group % 2


def device(x, y, z, core):
    return {"tile": (x % 2) * (Y * Z) + y * Z + z, "mode": (x // 2) * 2 + core}


def greet(partners):
    barrier = pltpu.get_barrier_semaphore()
    for partner in partners:
        pl.semaphore_signal(barrier, inc=1, device_id=partner, device_id_type=MESH)
    pl.semaphore_wait(barrier, len(partners))


def sender(send_sem, recv_sem):
    def make(index, src, dst, target):
        return pltpu.make_async_remote_copy(
            src_ref=src, dst_ref=dst, send_sem=send_sem.at[index], recv_sem=recv_sem.at[index],
            device_id=target, device_id_type=MESH,
        )
    return make


def gather_kernel(obj, probe, ext, modes, block, send_sem, recv_sem):
    tile, group, x, y, z, core = here()
    tiles = X * Y * Z // 2
    sibling = device(x, y, z, 1 - core)
    opposite = device((x + 2) % X, y, z, core)
    across = device(X - 1 - x, y, z, core)
    along_y = [device(x, (y + i) % Y, z, core) for i in (1, 3, 2)]
    before, after = (tile + tiles - 1) % tiles, (tile + 1) % tiles
    other = (group + 2) % 4
    halo_to = [
        {"tile": before, "mode": group}, {"tile": before, "mode": other},
        {"tile": after, "mode": group}, {"tile": after, "mode": other},
    ]
    block[...] = obj[...].astype(bf)
    for k in range(2):
        for c in range(2):
            modes[group, 2 * k + c] = probe[k, c].astype(bf)
    mine = pl.multiple_of(group * 128, 128)
    theirs = pl.multiple_of(other * 128, 128)
    ext[:, pl.ds(mine, 128), 128:640] = block[...]

    @pl.when(tile == 0)
    def _():
        ext[:, :, :128] = jnp.zeros((2, 512, 128), bf)

    @pl.when(tile == tiles - 1)
    def _():
        ext[:, :, 640:] = jnp.zeros((2, 512, 128), bf)

    greet([sibling, opposite, across] + along_y + halo_to)
    make = sender(send_sem, recv_sem)

    def rows(start, low, width):
        return ext.at[:, pl.ds(start, 128), pl.ds(low, width)]

    def plane(which, index):
        return modes.at[which, pl.ds(index, 1)]

    far = make(0, block, rows(mine, 128, 512), opposite)
    far.start()
    cut = make(1, plane(group, y), plane(group, y), across)
    cut.start()
    left, right = block.at[:, :, pl.ds(0, 128)], block.at[:, :, pl.ds(384, 128)]
    halo = [
        make(2, left, rows(mine, 640, 128), halo_to[0]),
        make(3, left, rows(mine, 640, 128), halo_to[1]),
        make(4, right, rows(mine, 0, 128), halo_to[2]),
        make(5, right, rows(mine, 0, 128), halo_to[3]),
    ]
    sends = (tile > 0, tile > 0, tile < tiles - 1, tile < tiles - 1)
    gets = (tile < tiles - 1, tile < tiles - 1, tile > 0, tile > 0)
    for flag, copy in zip(sends, halo):
        pl.when(flag)(copy.start)
    near = make(6, block, rows(mine, 128, 512), sibling)
    near.start()
    own = make(7, modes.at[group], modes.at[group], sibling)
    own.start()

    passed = []

    def pass_on(index, ref):
        copy = make(index, ref, ref, sibling)
        copy.start()
        passed.append(copy)

    cut.wait_recv()
    spread = []
    for i, target in enumerate(along_y):
        copy = make(8 + i, plane(other, y), plane(other, y), target)
        copy.start()
        spread.append(copy)
    pass_on(11, plane(other, y))
    halo_kept = []
    for i, (flag, start, low) in enumerate(
        zip(gets, (mine, theirs, mine, theirs), (640, 640, 0, 0))
    ):
        on = make(12 + i, rows(start, low, 128), rows(start, low, 128), sibling)
        halo_kept.append((flag, on))

        @pl.when(flag)
        def _():
            halo[i].wait_recv()
            on.start()
    far.wait_recv()
    pass_on(16, rows(theirs, 128, 512))
    for i, step in enumerate((1, 3, 2)):
        spread[i].wait_recv()
        pass_on(17 + i, plane(other, (y + Y - step) % Y))
    for copy in [near, own] + passed:
        copy.wait()
    for copy in [far, cut] + spread:
        copy.wait_send()
    for flag, copy in zip(sends, halo):
        pl.when(flag)(copy.wait_send)
    for flag, copy in halo_kept:
        pl.when(flag)(copy.wait)


def gather(obj, probe):
    whole = pl.BlockSpec(memory_space=pltpu.VMEM)
    return pl.pallas_call(
        gather_kernel,
        out_shape=(
            jax.ShapeDtypeStruct((2, 512, 768), bf), jax.ShapeDtypeStruct((4, 4, N, N), bf)
        ),
        in_specs=[whole, whole],
        out_specs=(whole, whole),
        scratch_shapes=[
            pltpu.VMEM((2, 128, 512), bf),
            pltpu.SemaphoreType.DMA((20,)), pltpu.SemaphoreType.DMA((20,)),
        ],
        compiler_params=pltpu.CompilerParams(
            collective_id=0, has_side_effects=True, vmem_limit_bytes=40 * 2**20
        ),
        name="gather",
    )(obj, probe)


def k2_kernel(rows, cols, live, ext, probe, meas, fwd, inv, grad, pg_out, pw,
              pg, ext32, patch, spec, gacc, light, UN=1):
    for c in range(2):
        ext32[c, :512, :768] = ext[c].astype(f32)
        ext32[c, :512, 768:] = jnp.zeros((512, 128), f32)
        ext32[c, 512:, :] = jnp.zeros((8, 896), f32)
    gacc[...] = jnp.zeros_like(gacc)
    pg[...] = jnp.zeros_like(pg)
    pw[...] = jnp.zeros_like(pw)
    light[...] = jnp.zeros_like(light)
    def lstep(m, _):
        re = probe[m, 0].astype(f32)
        im = probe[m, 1].astype(f32)
        light[...] += re * re + im * im
        return 0
    lax.fori_loop(0, 8, lstep, 0)

    def slot(s, _):
        @pl.when(live[s] > 0)
        def _():
            row = rows[s]
            col = cols[s]
            cb = pl.multiple_of((col // 128) * 128, 128)
            cr = col - cb
            back_shift = lax.rem(384 - cr, 384)
            rb = pl.multiple_of((row // 8) * 8, 8)
            rr = row - rb
            up = lax.rem(264 - rr, 264)
            for c in range(2):
                win = ext32[c, pl.ds(rb, 264), pl.ds(cb, 384)]
                win = pltpu.roll(win, back_shift, 1)[:, :N]
                patch[c] = pltpu.roll(win, up, 0)[:N]
            pw[...] += patch[0] * patch[0] + patch[1] * patch[1]

            def first(m, power):
                pr = probe[m, 0].astype(f32)
                pi = probe[m, 1].astype(f32)
                ar = patch[0]
                ai = patch[1]
                wave = jnp.concatenate([pr * ar - pi * ai, pr * ai + pi * ar], 1).astype(bf)
                half = dot(wave, fwd[...]).astype(bf)
                stacked = jnp.concatenate([half[:, :N], half[:, N:]], 0)
                sp = dot(inv[...], stacked)
                spec[m] = sp
                return power + sp[:N] * sp[:N] + sp[N:] * sp[N:]
            power = lax.fori_loop(0, 8, first, jnp.zeros((N, N), f32), unroll=UN)
            factor = meas[s] * lax.rsqrt(jnp.maximum(power, 0.25)) - 1.0
            patch[2] = factor

            def second(m, carry):
                gr, gi = carry
                fac = patch[2]
                sp = spec[m]
                diff = jnp.concatenate([sp[:N] * fac, sp[N:] * fac], 0).astype(bf)
                bh = dot(fwd[...], diff).astype(bf)
                wide = jnp.concatenate([bh[:N], bh[N:]], 1)
                back = dot(wide, inv[...])
                br = back[:, :N]
                bi = back[:, N:]
                pr = probe[m, 0].astype(f32)
                pi = probe[m, 1].astype(f32)
                ar = patch[0]
                ai = patch[1]
                pg[m, 0] += ar * br + ai * bi
                pg[m, 1] += ar * bi - ai * br
                return gr + pr * br + pi * bi, gi + pr * bi - pi * br
            z = jnp.zeros((N, N), f32)
            gr, gi = lax.fori_loop(0, 8, second, (z, z), unroll=UN)
            pad = jnp.zeros((N, 128), f32)
            low = jnp.zeros((8, 384), f32)
            for c, term in enumerate((gr, gi, light[...])):
                moved = pltpu.roll(jnp.concatenate([term, pad], 1), cr, 1)
                moved = pltpu.roll(jnp.concatenate([moved, low], 0), rr, 0)
                gacc[c, pl.ds(rb, 264), pl.ds(cb, 384)] += moved
        return 0
    lax.fori_loop(0, 3, slot, 0)
    grad[...] = gacc[:, :512, :768]
    pg_out[...] = pg[...].astype(bf)

def k2(rows, cols, live, ext, probe, meas, UN=1):
    fwd, inv = tables()
    probe = probe.reshape(8, 2, N, N)
    V = pl.BlockSpec(memory_space=pltpu.VMEM)
    S = pl.BlockSpec(memory_space=pltpu.SMEM)
    return pl.pallas_call(
        functools.partial(k2_kernel, UN=UN),
        out_shape=(jax.ShapeDtypeStruct((3, 512, 768), f32),
                   jax.ShapeDtypeStruct((8, 2, N, N), bf),
                   jax.ShapeDtypeStruct((N, N), f32)),
        in_specs=[S, S, S, V, V, V, V, V],
        out_specs=(V, V, V),
        scratch_shapes=[pltpu.VMEM((8, 2, N, N), f32), pltpu.VMEM((2, 520, 896), f32), pltpu.VMEM((3, N, N), f32),
                        pltpu.VMEM((8, 512, N), f32), pltpu.VMEM((3, 520, 896), f32), pltpu.VMEM((N, N), f32)],
        compiler_params=pltpu.CompilerParams(vmem_limit_bytes=60 * 2**20),
        name="refine",
    )(rows, cols, live, ext, probe, meas, jnp.asarray(fwd), jnp.asarray(inv))


def spread_kernel(grad, probe_sum, power, obj, probe_rows, object_out, probe_out,
                  sent_power, got_obj, got_probe, got_power, out_obj, out_halo, got_center, got_halo,
                  pieces, got_piece, bands, got_band, send_sem, recv_sem):
    tile, group, x, y, z, core = here()
    tiles = X * Y * Z // 2
    x_hi = group // 2
    sibling = device(x, y, z, 1 - core)
    opposite = device((x + 2) % X, y, z, core)
    before, after = (tile + tiles - 1) % tiles, (tile + 1) % tiles
    other = (group + 2) % 4
    halo_to = [
        {"tile": before, "mode": group}, {"tile": before, "mode": other},
        {"tile": after, "mode": group}, {"tile": after, "mode": other},
    ]
    in_plane = [device((x + i) % X, (y + j) % Y, z, core) for i, j in XY]
    along_z = [device(x, y, (z + i) % Z, core) for i in range(1, Z)]
    make = sender(send_sem, recv_sem)

    sent_power[...] = power[...].astype(bf)
    greet([sibling] + halo_to + in_plane + along_z)

    first = []
    for h in range(2):
        start = pl.multiple_of((2 * h + 1 - core) * 128, 128)
        first.append(make(h, probe_sum.at[2 * h + 1 - core], got_probe.at[h], sibling))
        first.append(make(2 + h, grad.at[:, pl.ds(start, 128), :], got_obj.at[h], sibling))
    first.append(make(4, sent_power, got_power, sibling))
    for copy in first:
        copy.start()
    for i in (0, 2, 4):
        first[i].wait_recv()
    total_power = (sent_power[...].astype(f32) + got_power[...].astype(f32)).astype(bf)
    for h in range(2):
        pieces[h, 4] = total_power
        for k in range(4):
            pieces[h, k] = (
                probe_sum[2 * h + core, k].astype(f32) + got_probe[h, k].astype(f32)
            ).astype(bf)

    def band(px, py):
        start = pl.multiple_of((px % 2) * 128 + py * 32, 32)
        return pieces.at[px // 2, :, pl.ds(start, 32), :]

    second = []
    for k, (i, j) in enumerate(XY):
        copy = make(5 + k, band((x + i) % X, (y + j) % Y), got_piece.at[k], in_plane[k])
        copy.start()
        second.append(copy)

    first[1].wait_recv()
    first[3].wait_recv()
    mine = pl.multiple_of(group * 128, 128)
    theirs = pl.multiple_of(other * 128, 128)
    for k in range(3):
        out_obj[k] = (grad[k, pl.ds(theirs, 128), :] + got_obj[1 - x_hi, k]).astype(bf)
        out_halo[0, k] = (grad[k, pl.ds(mine, 128), :128] + got_obj[x_hi, k, :, :128]).astype(bf)
        out_halo[1, k] = (grad[k, pl.ds(mine, 128), 640:] + got_obj[x_hi, k, :, 640:]).astype(bf)
    third = [
        make(20, out_obj.at[:, :, pl.ds(128, 512)], got_center, opposite),
        make(21, out_halo.at[0], got_halo.at[0], halo_to[0]),
        make(22, out_obj.at[:, :, pl.ds(0, 128)], got_halo.at[1], halo_to[1]),
        make(23, out_halo.at[1], got_halo.at[2], halo_to[2]),
        make(24, out_obj.at[:, :, pl.ds(640, 128)], got_halo.at[3], halo_to[3]),
    ]
    for copy in third:
        copy.start()

    start = pl.multiple_of((x % 2) * 128 + y * 32, 32)
    total = pieces[x_hi, :, pl.ds(start, 32), :].astype(f32)
    for k in range(len(XY)):
        second[k].wait_recv()
        total = total + got_piece[k].astype(f32)
    for part in range(Z):
        for k in range(5):
            bands[part, 4 * k:4 * k + 4] = total[k, 4 * part:4 * part + 4]
    fourth = []
    for i in range(1, Z):
        copy = make(24 + i, bands.at[(z + i) % Z], got_band.at[i - 1], along_z[i - 1])
        copy.start()
        fourth.append(copy)

    for copy in third:
        copy.wait_recv()
    keep_left = jnp.where(tile > 0, 1.0, 0.0)
    keep_right = jnp.where(tile < tiles - 1, 1.0, 0.0)
    parts = []
    for k in range(3):
        center = grad[k, pl.ds(mine, 128), 128:640] + got_obj[x_hi, k, :, 128:640]
        center = center + got_center[k].astype(f32)
        from_right = (got_halo[0, k].astype(f32) + got_halo[1, k].astype(f32)) * keep_right
        from_left = (got_halo[2, k].astype(f32) + got_halo[3, k].astype(f32)) * keep_left
        parts.append(jnp.concatenate(
            [center[:, :128] + from_left, center[:, 128:384], center[:, 384:] + from_right], 1
        ))
    for k in range(2):
        object_out[k] = obj[k] + parts[k] / (parts[2] + object_reg)

    final = bands[z]
    for i in range(Z - 1):
        fourth[i].wait_recv()
        final = final + got_band[i]
    weight = final[16:20] + probe_reg
    for k in range(4):
        probe_out[k] = probe_rows[k] + final[4 * k:4 * k + 4] / weight
    for copy in first + second + third + fourth:
        copy.wait_send()


def spread(grad, probe_sum, power, obj, probe_rows):
    whole = pl.BlockSpec(memory_space=pltpu.VMEM)
    return pl.pallas_call(
        spread_kernel,
        out_shape=(
            jax.ShapeDtypeStruct((2, 128, 512), f32), jax.ShapeDtypeStruct((4, 4, N), f32)
        ),
        in_specs=[whole] * 5,
        out_specs=(whole, whole),
        scratch_shapes=[
            pltpu.VMEM((N, N), bf),
            pltpu.VMEM((2, 3, 128, 768), f32),
            pltpu.VMEM((2, 4, N, N), bf),
            pltpu.VMEM((N, N), bf),
            pltpu.VMEM((3, 128, 768), bf),
            pltpu.VMEM((2, 3, 128, 128), bf),
            pltpu.VMEM((3, 128, 512), bf),
            pltpu.VMEM((4, 3, 128, 128), bf),
            pltpu.VMEM((2, 5, N, N), bf),
            pltpu.VMEM((len(XY), 5, 32, N), bf),
            pltpu.VMEM((Z, 24, N), f32),
            pltpu.VMEM((Z - 1, 24, N), f32),
            pltpu.SemaphoreType.DMA((32,)), pltpu.SemaphoreType.DMA((32,)),
        ],
        compiler_params=pltpu.CompilerParams(
            collective_id=1, has_side_effects=True, vmem_limit_bytes=50 * 2**20
        ),
        name="spread",
    )(grad, probe_sum, power, obj, probe_rows)


def local(object_field, probe, measured, scan_rows, scan_cols, counts):
    slots = scan_rows.shape[0]
    first_slot = lax.axis_index("mode") * slots
    live = (first_slot + jnp.arange(slots, dtype=jnp.int32) < counts[0]).astype(jnp.int32)
    extended, probe_all = gather(object_field, probe)
    gradient, probe_sum, power = k2(
        scan_rows, scan_cols, live, extended, probe_all, measured, UN=2
    )
    probe_rows = lax.dynamic_slice_in_dim(probe, lax.axis_index("tile") * 4, 4, 2)
    object_out, probe_out = spread(
        gradient, probe_sum.reshape(4, 4, N, N), power, object_field, probe_rows.reshape(4, 4, N)
    )
    return object_out, probe_out.reshape(2, 2, 4, N)


def solution(mesh):
    return jax.shard_map(
        local,
        mesh=mesh,
        in_specs=(
            P(None, "mode", "tile"),
            P("mode", None, None, None),
            P(("tile", "mode"), None, None),
            P(("tile", "mode")),
            P(("tile", "mode")),
            P("tile"),
        ),
        out_specs=(P(None, "mode", "tile"), P("mode", None, "tile", None)),
        check_vma=False,
    )
```

```python
import functools

import jax
import jax.numpy as jnp
import ml_dtypes
import numpy as np
from jax import lax
from jax.experimental import pallas as pl
from jax.experimental.pallas import tpu as pltpu
from jax.sharding import PartitionSpec as P

object_reg = 0.5
probe_reg = 1.0
N = 256
X, Y, Z = 4, 4, 8
bf = jnp.bfloat16
f32 = jnp.float32
MESH = pl.DeviceIdType.MESH
XY = [(i, j) for i in range(X) for j in range(Y) if i or j]


def tables():
    pos = np.arange(N)
    ang = (pos[:, None] * pos[None, :] % N) * (2.0 * np.pi / N)
    sc = 1.0 / np.sqrt(float(N))
    re = (np.cos(ang) * sc).astype(ml_dtypes.bfloat16)
    im = (-np.sin(ang) * sc).astype(ml_dtypes.bfloat16)
    forward = np.block([[re, im], [-im, re]]).astype(ml_dtypes.bfloat16)
    inverse = np.block([[re, -im], [im, re]]).astype(ml_dtypes.bfloat16)
    return forward, inverse


def dot(a, b):
    return jnp.dot(a, b, preferred_element_type=f32)


def here():
    tile = lax.axis_index("tile")
    group = lax.axis_index("mode")
    x = (group // 2) * 2 + tile // (Y * Z)
    return tile, group, x, (tile // Z) % Y, tile % Z, group % 2


def device(x, y, z, core):
    return {"tile": (x % 2) * (Y * Z) + y * Z + z, "mode": (x // 2) * 2 + core}


def greet(partners):
    barrier = pltpu.get_barrier_semaphore()
    for partner in partners:
        pl.semaphore_signal(barrier, inc=1, device_id=partner, device_id_type=MESH)
    pl.semaphore_wait(barrier, len(partners))


def sender(send_sem, recv_sem):
    def make(index, src, dst, target):
        return pltpu.make_async_remote_copy(
            src_ref=src, dst_ref=dst, send_sem=send_sem.at[index], recv_sem=recv_sem.at[index],
            device_id=target, device_id_type=MESH,
        )
    return make


def gather_kernel(obj, probe, ext, modes, block, send_sem, recv_sem):
    tile, group, x, y, z, core = here()
    tiles = X * Y * Z // 2
    sibling = device(x, y, z, 1 - core)
    opposite = device((x + 2) % X, y, z, core)
    across = device(X - 1 - x, y, z, core)
    along_y = [device(x, (y + i) % Y, z, core) for i in (1, 3, 2)]
    before, after = (tile + tiles - 1) % tiles, (tile + 1) % tiles
    other = (group + 2) % 4
    halo_to = [
        {"tile": before, "mode": group}, {"tile": before, "mode": other},
        {"tile": after, "mode": group}, {"tile": after, "mode": other},
    ]
    block[...] = obj[...].astype(bf)
    for k in range(2):
        for c in range(2):
            modes[group, 2 * k + c] = probe[k, c].astype(bf)
    mine = pl.multiple_of(group * 128, 128)
    theirs = pl.multiple_of(other * 128, 128)
    ext[:, pl.ds(mine, 128), 128:640] = block[...]

    @pl.when(tile == 0)
    def _():
        ext[:, :, :128] = jnp.zeros((2, 512, 128), bf)

    @pl.when(tile == tiles - 1)
    def _():
        ext[:, :, 640:] = jnp.zeros((2, 512, 128), bf)

    greet([sibling, opposite, across] + along_y + halo_to)
    make = sender(send_sem, recv_sem)

    def rows(start, low, width):
        return ext.at[:, pl.ds(start, 128), pl.ds(low, width)]

    def plane(which, index):
        return modes.at[which, pl.ds(index, 1)]

    far = make(0, block, rows(mine, 128, 512), opposite)
    far.start()
    cut = make(1, plane(group, y), plane(group, y), across)
    cut.start()
    left, right = block.at[:, :, pl.ds(0, 128)], block.at[:, :, pl.ds(384, 128)]
    halo = [
        make(2, left, rows(mine, 640, 128), halo_to[0]),
        make(3, left, rows(mine, 640, 128), halo_to[1]),
        make(4, right, rows(mine, 0, 128), halo_to[2]),
        make(5, right, rows(mine, 0, 128), halo_to[3]),
    ]
    sends = (tile > 0, tile > 0, tile < tiles - 1, tile < tiles - 1)
    gets = (tile < tiles - 1, tile < tiles - 1, tile > 0, tile > 0)
    for flag, copy in zip(sends, halo):
        pl.when(flag)(copy.start)
    near = make(6, block, rows(mine, 128, 512), sibling)
    near.start()
    own = make(7, modes.at[group], modes.at[group], sibling)
    own.start()

    passed = []

    def pass_on(index, ref):
        copy = make(index, ref, ref, sibling)
        copy.start()
        passed.append(copy)

    cut.wait_recv()
    spread = []
    for i, target in enumerate(along_y):
        copy = make(8 + i, plane(other, y), plane(other, y), target)
        copy.start()
        spread.append(copy)
    pass_on(11, plane(other, y))
    halo_kept = []
    for i, (flag, start, low) in enumerate(
        zip(gets, (mine, theirs, mine, theirs), (640, 640, 0, 0))
    ):
        on = make(12 + i, rows(start, low, 128), rows(start, low, 128), sibling)
        halo_kept.append((flag, on))

        @pl.when(flag)
        def _():
            halo[i].wait_recv()
            on.start()
    far.wait_recv()
    pass_on(16, rows(theirs, 128, 512))
    for i, step in enumerate((1, 3, 2)):
        spread[i].wait_recv()
        pass_on(17 + i, plane(other, (y + Y - step) % Y))
    for copy in [near, own] + passed:
        copy.wait()
    for copy in [far, cut] + spread:
        copy.wait_send()
    for flag, copy in zip(sends, halo):
        pl.when(flag)(copy.wait_send)
    for flag, copy in halo_kept:
        pl.when(flag)(copy.wait)


def gather(obj, probe):
    whole = pl.BlockSpec(memory_space=pltpu.VMEM)
    return pl.pallas_call(
        gather_kernel,
        out_shape=(
            jax.ShapeDtypeStruct((2, 512, 768), bf), jax.ShapeDtypeStruct((4, 4, N, N), bf)
        ),
        in_specs=[whole, whole],
        out_specs=(whole, whole),
        scratch_shapes=[
            pltpu.VMEM((2, 128, 512), bf),
            pltpu.SemaphoreType.DMA((20,)), pltpu.SemaphoreType.DMA((20,)),
        ],
        compiler_params=pltpu.CompilerParams(
            collective_id=0, has_side_effects=True, vmem_limit_bytes=40 * 2**20
        ),
        name="gather",
    )(obj, probe)


def refine_kernel(rows, cols, ext, probe, meas, fwd, inv, obj, probe_rows, object_out, probe_out,
                  patch, factor, spec, light, terms, to_cols, total, grads, sums,
                  out_probe, got_probe, out_power, got_power, pieces, got_piece, bands, got_band,
                  out_light, got_light, far_light, far_got_light, halo_light, halo_got_light,
                  out_grad, got_grad, far_grad, far_got_grad, halo_grad, halo_got_grad,
                  send_sem, recv_sem):
    tile, group, x, y, z, core = here()
    tiles = X * Y * Z // 2
    x_hi = group // 2
    sibling = device(x, y, z, 1 - core)
    opposite = device((x + 2) % X, y, z, core)
    before, after = (tile + tiles - 1) % tiles, (tile + 1) % tiles
    other = (group + 2) % 4
    halo_to = [
        {"tile": before, "mode": group}, {"tile": before, "mode": other},
        {"tile": after, "mode": group}, {"tile": after, "mode": other},
    ]
    in_plane = [device((x + i) % X, (y + j) % Y, z, core) for i, j in XY]
    along_z = [device(x, y, (z + i) % Z, core) for i in range(1, Z)]
    make = sender(send_sem, recv_sem)
    slots = 3

    greet([sibling] + halo_to + in_plane + along_z)

    light[...] = jnp.zeros_like(light)
    factor[0] = jnp.zeros((N, N), f32)

    def picks(height, width, shift, down):
        high = lax.broadcasted_iota(jnp.int32, (height, width), 0)
        wide = lax.broadcasted_iota(jnp.int32, (height, width), 1)
        hit = high == wide + shift if down else wide == high + shift
        return jnp.where(hit, 1.0, 0.0).astype(bf)

    def mode_light(g, _):
        for k in range(2):
            re = probe[g, 2 * k].astype(f32)
            im = probe[g, 2 * k + 1].astype(f32)
            light[...] += re * re + im * im
        return 0
    lax.fori_loop(0, 4, mode_light, 0)

    def scatter(c):
        spread_rows = [
            dot(picks(512, N, rows[s], True), terms[s]).astype(bf) for s in range(slots)
        ]
        for s in range(slots):
            to_cols[s * N:(s + 1) * N, :] = picks(N, 768, cols[s], False)
        total[c] = dot(jnp.concatenate(spread_rows, 1), to_cols[...])

    for s in range(slots):
        from_cols = picks(768, N, cols[s], True)
        from_rows = picks(N, 512, rows[s], False)
        for c in range(2):
            strip = dot(ext[c], from_cols).astype(bf)
            patch[s, c] = dot(from_rows, strip)
        factor[0] += patch[s, 0] * patch[s, 0] + patch[s, 1] * patch[s, 1]
        terms[s] = light[...].astype(bf)
    scatter(0)
    out_power[...] = factor[0].astype(bf)
    power_copy = make(0, out_power, got_power, sibling)
    power_copy.start()

    def sibling_rows(c, out, k):
        for h in range(2):
            start = pl.multiple_of((2 * h + 1 - core) * 128, 128)
            out[h, k] = total[c, pl.ds(start, 128), :].astype(bf)

    def own_rows(c, h, got, k):
        start = pl.multiple_of((2 * h + core) * 128, 128)
        return total[c, pl.ds(start, 128), :] + got[h, k].astype(f32)

    def fan_out(first, far, far_got, halo, halo_got):
        copies = [
            make(first, far.at[:, :, pl.ds(128, 512)], far_got, opposite),
            make(first + 1, halo.at[0], halo_got.at[0], halo_to[0]),
            make(first + 2, far.at[:, :, pl.ds(0, 128)], halo_got.at[1], halo_to[1]),
            make(first + 3, halo.at[1], halo_got.at[2], halo_to[2]),
            make(first + 4, far.at[:, :, pl.ds(640, 128)], halo_got.at[3], halo_to[3]),
        ]
        for copy in copies:
            copy.start()
        return copies

    keep_left = jnp.where(tile > 0, 1.0, 0.0)
    keep_right = jnp.where(tile < tiles - 1, 1.0, 0.0)

    def merged(kept, far_got, halo_got, k):
        center = kept[:, 128:640] + far_got[k].astype(f32)
        from_right = (halo_got[0, k].astype(f32) + halo_got[1, k].astype(f32)) * keep_right
        from_left = (halo_got[2, k].astype(f32) + halo_got[3, k].astype(f32)) * keep_left
        return jnp.concatenate(
            [center[:, :128] + from_left, center[:, 128:384], center[:, 384:] + from_right], 1
        )

    sibling_rows(0, out_light, 0)
    light_copy = make(1, out_light, got_light, sibling)
    light_copy.start()

    def spectra(s, _):
        power = jnp.zeros((N, N), f32)
        ar = patch[s, 0]
        ai = patch[s, 1]
        for m in range(8):
            pr = probe[m // 2, 2 * (m % 2)].astype(f32)
            pi = probe[m // 2, 2 * (m % 2) + 1].astype(f32)
            wave = jnp.concatenate([pr * ar - pi * ai, pr * ai + pi * ar], 1).astype(bf)
            half = dot(wave, fwd[...]).astype(bf)
            spectrum = dot(inv[...], jnp.concatenate([half[:, :N], half[:, N:]], 0))
            spec[s, m] = spectrum
            power = power + spectrum[:N] * spectrum[:N] + spectrum[N:] * spectrum[N:]
        factor[s] = meas[s] * lax.rsqrt(jnp.maximum(power, 0.25)) - 1.0
        return 0
    lax.fori_loop(0, slots, spectra, 0)

    light_copy.wait_recv()
    kept_light = own_rows(0, x_hi, got_light, 0)
    far_light[0] = own_rows(0, 1 - x_hi, got_light, 0).astype(bf)
    halo_light[0, 0] = kept_light[:, :128].astype(bf)
    halo_light[1, 0] = kept_light[:, 640:].astype(bf)
    light_copies = fan_out(2, far_light, far_got_light, halo_light, halo_got_light)
    power_copy.wait_recv()
    total_power = (out_power[...].astype(f32) + got_power[...].astype(f32)).astype(bf)
    pieces[0, 4] = total_power
    pieces[1, 4] = total_power

    grads[...] = jnp.zeros_like(grads)

    def passed(q):
        return make(7 + q, out_probe.at[q], got_probe.at[q], sibling)

    def piece(h, xl, j):
        i = (2 * h + xl - x + X) % X
        k = i * Y + j
        start = pl.multiple_of(xl * 128 + ((y + j) % Y) * 32, 32)
        copy = make(
            9 + k, pieces.at[h, :, pl.ds(start, 32), :], got_piece.at[k],
            device(2 * h + xl, (y + j) % Y, z, core),
        )
        return copy, k

    def back_step(q, _):
        h = q % 2
        side = jnp.where(q < 2, 1 - core, core)
        g = 2 * h + side
        sums[...] = jnp.zeros_like(sums)
        for s in range(slots):
            fac = factor[s]
            ar = patch[s, 0]
            ai = patch[s, 1]
            for k in range(2):
                spectrum = spec[s, 2 * g + k]
                diff = jnp.concatenate([spectrum[:N] * fac, spectrum[N:] * fac], 0).astype(bf)
                half = dot(fwd[...], diff).astype(bf)
                back = dot(jnp.concatenate([half[:N], half[N:]], 1), inv[...])
                br = back[:, :N]
                bi = back[:, N:]
                pr = probe[g, 2 * k].astype(f32)
                pi = probe[g, 2 * k + 1].astype(f32)
                sums[2 * k] += ar * br + ai * bi
                sums[2 * k + 1] += ar * bi - ai * br
                grads[s, 0] += pr * br + pi * bi
                grads[s, 1] += pr * bi - pi * br

        @pl.when(q < 2)
        def _():
            out_probe[h] = sums[...].astype(bf)
            passed(h).start()

        @pl.when(q >= 2)
        def _():
            passed(h).wait_recv()
            for k in range(4):
                pieces[h, k] = (sums[k] + got_probe[h, k].astype(f32)).astype(bf)
            for xl in range(2):
                for j in range(Y):
                    copy, k = piece(h, xl, j)
                    if j:
                        copy.start()
                    else:
                        pl.when(k > 0)(copy.start)
        return 0
    lax.fori_loop(0, 4, back_step, 0)

    for copy in light_copies:
        copy.wait_recv()
    weight = merged(kept_light, far_got_light, halo_got_light, 0) + object_reg

    for c in range(2):
        for s in range(slots):
            terms[s] = grads[s, c].astype(bf)
        scatter(c)
    for c in range(2):
        sibling_rows(c, out_grad, c)
    grad_copy = make(32, out_grad, got_grad, sibling)
    grad_copy.start()

    band_start = pl.multiple_of((x % 2) * 128 + y * 32, 32)
    band = pieces[x_hi, :, pl.ds(band_start, 32), :].astype(f32)
    grad_copy.wait_recv()
    for c in range(2):
        far_grad[c] = own_rows(c, 1 - x_hi, got_grad, c).astype(bf)
        halo_grad[0, c] = own_rows(c, x_hi, got_grad, c)[:, :128].astype(bf)
        halo_grad[1, c] = own_rows(c, x_hi, got_grad, c)[:, 640:].astype(bf)
    grad_copies = fan_out(33, far_grad, far_got_grad, halo_grad, halo_got_grad)

    def arrived(k):
        return make(9 + k, pieces.at[0, :, pl.ds(0, 32), :], got_piece.at[k], sibling)
    for k in range(1, X * Y):
        arrived(k).wait_recv()
        band = band + got_piece[k].astype(f32)
    for part in range(Z):
        for k in range(5):
            bands[part, 4 * k:4 * k + 4] = band[k, 4 * part:4 * part + 4]
    band_copies = []
    for i in range(1, Z):
        copy = make(24 + i, bands.at[(z + i) % Z], got_band.at[i - 1], along_z[i - 1])
        copy.start()
        band_copies.append(copy)

    for copy in grad_copies:
        copy.wait_recv()
    for c in range(2):
        kept = own_rows(c, x_hi, got_grad, c)
        object_out[c] = obj[c] + merged(kept, far_got_grad, halo_got_grad, c) / weight

    final = bands[z]
    for i in range(Z - 1):
        band_copies[i].wait_recv()
        final = final + got_band[i]
    weight = final[16:20] + probe_reg
    for k in range(4):
        probe_out[k] = probe_rows[k] + final[4 * k:4 * k + 4] / weight
    for copy in [power_copy, light_copy, grad_copy, passed(0), passed(1)] + light_copies + grad_copies + band_copies:
        copy.wait_send()
    for k in range(1, X * Y):
        arrived(k).wait_send()


def refine(rows, cols, ext, probe, meas, obj, probe_rows):
    forward, inverse = tables()
    whole = pl.BlockSpec(memory_space=pltpu.VMEM)
    scalars = pl.BlockSpec(memory_space=pltpu.SMEM)
    return pl.pallas_call(
        refine_kernel,
        out_shape=(
            jax.ShapeDtypeStruct((2, 128, 512), f32), jax.ShapeDtypeStruct((4, 4, N), f32)
        ),
        in_specs=[scalars] * 2 + [whole] * 7,
        out_specs=(whole, whole),
        scratch_shapes=[
            pltpu.VMEM((3, 2, N, N), f32),
            pltpu.VMEM((3, N, N), f32),
            pltpu.VMEM((3, 8, 2 * N, N), f32),
            pltpu.VMEM((N, N), f32),
            pltpu.VMEM((3, N, N), bf),
            pltpu.VMEM((3 * N, 768), bf),
            pltpu.VMEM((2, 512, 768), f32),
            pltpu.VMEM((3, 2, N, N), f32),
            pltpu.VMEM((4, N, N), f32),
            pltpu.VMEM((2, 4, N, N), bf),
            pltpu.VMEM((2, 4, N, N), bf),
            pltpu.VMEM((N, N), bf),
            pltpu.VMEM((N, N), bf),
            pltpu.VMEM((2, 5, N, N), bf),
            pltpu.VMEM((X * Y, 5, 32, N), bf),
            pltpu.VMEM((Z, 24, N), f32),
            pltpu.VMEM((Z - 1, 24, N), f32),
            pltpu.VMEM((2, 1, 128, 768), bf),
            pltpu.VMEM((2, 1, 128, 768), bf),
            pltpu.VMEM((1, 128, 768), bf),
            pltpu.VMEM((1, 128, 512), bf),
            pltpu.VMEM((2, 1, 128, 128), bf),
            pltpu.VMEM((4, 1, 128, 128), bf),
            pltpu.VMEM((2, 2, 128, 768), bf),
            pltpu.VMEM((2, 2, 128, 768), bf),
            pltpu.VMEM((2, 128, 768), bf),
            pltpu.VMEM((2, 128, 512), bf),
            pltpu.VMEM((2, 2, 128, 128), bf),
            pltpu.VMEM((4, 2, 128, 128), bf),
            pltpu.SemaphoreType.DMA((40,)), pltpu.SemaphoreType.DMA((40,)),
        ],
        compiler_params=pltpu.CompilerParams(
            collective_id=1, has_side_effects=True, vmem_limit_bytes=60 * 2**20
        ),
        name="refine",
    )(rows, cols, ext, probe, meas, jnp.asarray(forward), jnp.asarray(inverse), obj, probe_rows)


def local(object_field, probe, measured, scan_rows, scan_cols, counts):
    slots = scan_rows.shape[0]
    first_slot = lax.axis_index("mode") * slots
    live = first_slot + jnp.arange(slots, dtype=jnp.int32) < counts[0]
    live_rows = jnp.where(live, scan_rows, 4096)
    extended, probe_all = gather(object_field, probe)
    probe_rows = lax.dynamic_slice_in_dim(probe, lax.axis_index("tile") * 4, 4, 2)
    object_out, probe_out = refine(
        live_rows, scan_cols, extended, probe_all, measured, object_field,
        probe_rows.reshape(4, 4, N),
    )
    return object_out, probe_out.reshape(2, 2, 4, N)


def solution(mesh):
    return jax.shard_map(
        local,
        mesh=mesh,
        in_specs=(
            P(None, "mode", "tile"),
            P("mode", None, None, None),
            P(("tile", "mode"), None, None),
            P(("tile", "mode")),
            P(("tile", "mode")),
            P("tile"),
        ),
        out_specs=(P(None, "mode", "tile"), P("mode", None, "tile", None)),
        check_vma=False,
    )
```

```python
import functools

import jax
import jax.numpy as jnp
import ml_dtypes
import numpy as np
from jax import lax
from jax.experimental import pallas as pl
from jax.experimental.pallas import tpu as pltpu
from jax.sharding import PartitionSpec as P

object_reg = 0.5
probe_reg = 1.0
N = 256
X, Y, Z = 4, 4, 8
bf = jnp.bfloat16
f32 = jnp.float32
MESH = pl.DeviceIdType.MESH
XY = [(i, j) for i in range(X) for j in range(Y) if i or j]


def tables():
    pos = np.arange(N)
    ang = (pos[:, None] * pos[None, :] % N) * (2.0 * np.pi / N)
    sc = 1.0 / np.sqrt(float(N))
    re = (np.cos(ang) * sc).astype(ml_dtypes.bfloat16)
    im = (-np.sin(ang) * sc).astype(ml_dtypes.bfloat16)
    forward = np.block([[re, im], [-im, re]]).astype(ml_dtypes.bfloat16)
    inverse = np.block([[re, -im], [im, re]]).astype(ml_dtypes.bfloat16)
    return forward, inverse


def dot(a, b):
    return jnp.dot(a, b, preferred_element_type=f32)


def here():
    tile = lax.axis_index("tile")
    group = lax.axis_index("mode")
    x = (group // 2) * 2 + tile // (Y * Z)
    return tile, group, x, (tile // Z) % Y, tile % Z, group % 2


def device(x, y, z, core):
    return {"tile": (x % 2) * (Y * Z) + y * Z + z, "mode": (x // 2) * 2 + core}


def greet(partners):
    barrier = pltpu.get_barrier_semaphore()
    for partner in partners:
        pl.semaphore_signal(barrier, inc=1, device_id=partner, device_id_type=MESH)
    pl.semaphore_wait(barrier, len(partners))


def sender(send_sem, recv_sem):
    def make(index, src, dst, target):
        return pltpu.make_async_remote_copy(
            src_ref=src, dst_ref=dst, send_sem=send_sem.at[index], recv_sem=recv_sem.at[index],
            device_id=target, device_id_type=MESH,
        )
    return make


def refine_kernel(counts, rows_in, cols, obj_in, probe_in, meas_in, fwd_in, inv_in, object_out, probe_out,
                  obj, probe, meas, fwd, inv, block, ext, modes, powers,
                  patch, factor, spec, light, terms, to_cols, total, grads, sums,
                  out_probe, got_probe, out_power, got_power, pieces, got_piece, bands, got_band,
                  out_light, got_light, far_light, far_got_light, halo_light, halo_got_light,
                  out_grad, got_grad, far_grad, far_got_grad, halo_grad, halo_got_grad,
                  send_sem, recv_sem, load_sem):
    loads = [
        pltpu.make_async_copy(src, dst, load_sem.at[i])
        for i, (src, dst) in enumerate(
            ((obj_in, obj), (probe_in, probe), (fwd_in, fwd), (inv_in, inv), (meas_in, meas))
        )
    ]
    for load in loads:
        load.start()
    slots = 3
    tile, group, x, y, z, core = here()
    tiles = X * Y * Z // 2
    x_hi = group // 2
    sibling = device(x, y, z, 1 - core)
    opposite = device((x + 2) % X, y, z, core)
    before, after = (tile + tiles - 1) % tiles, (tile + 1) % tiles
    other = (group + 2) % 4
    halo_to = [
        {"tile": before, "mode": group}, {"tile": before, "mode": other},
        {"tile": after, "mode": group}, {"tile": after, "mode": other},
    ]
    in_plane = [device((x + i) % X, (y + j) % Y, z, core) for i, j in XY]
    along_z = [device(x, y, (z + i) % Z, core) for i in range(1, Z)]
    make = sender(send_sem, recv_sem)

    across = device(X - 1 - x, y, z, core)
    along_y = [device(x, (y + i) % Y, z, core) for i in (1, 3, 2)]
    partners = [sibling] + halo_to + in_plane + along_z
    barrier = pltpu.get_barrier_semaphore()
    for partner in partners:
        pl.semaphore_signal(barrier, inc=1, device_id=partner, device_id_type=MESH)
    rows = [jnp.where(group * slots + s < counts[0], rows_in[s], 4096) for s in range(slots)]

    mine = pl.multiple_of(group * 128, 128)
    theirs = pl.multiple_of(other * 128, 128)
    loads[0].wait()
    block[...] = obj[...].astype(bf)
    ext[:, pl.ds(mine, 128), 128:640] = block[...]

    @pl.when(tile == 0)
    def _():
        ext[:, :, :128] = jnp.zeros((2, 512, 128), bf)

    @pl.when(tile == tiles - 1)
    def _():
        ext[:, :, 640:] = jnp.zeros((2, 512, 128), bf)

    loads[1].wait()
    for k in range(2):
        for c in range(2):
            modes[group, 2 * k + c] = probe[k, c].astype(bf)
    pl.semaphore_wait(barrier, len(partners))

    def strip(start, low, width):
        return ext.at[:, pl.ds(start, 128), pl.ds(low, width)]

    def plane(which, index):
        return modes.at[which, pl.ds(index, 1)]

    far = make(40, block, strip(mine, 128, 512), opposite)
    far.start()
    left, right = block.at[:, :, pl.ds(0, 128)], block.at[:, :, pl.ds(384, 128)]
    halo = [
        make(42, left, strip(mine, 640, 128), halo_to[0]),
        make(43, left, strip(mine, 640, 128), halo_to[1]),
        make(44, right, strip(mine, 0, 128), halo_to[2]),
        make(45, right, strip(mine, 0, 128), halo_to[3]),
    ]
    sends = (tile > 0, tile > 0, tile < tiles - 1, tile < tiles - 1)
    gets = (tile < tiles - 1, tile < tiles - 1, tile > 0, tile > 0)
    for flag, copy in zip(sends, halo):
        pl.when(flag)(copy.start)
    cut = make(41, plane(group, y), plane(group, y), across)
    cut.start()
    near = make(46, block, strip(mine, 128, 512), sibling)
    near.start()
    own = make(47, modes.at[group], modes.at[group], sibling)
    own.start()

    def pass_on(index, ref):
        copy = make(index, ref, ref, sibling)
        copy.start()
        return copy

    halo_kept = []
    for i, (flag, start, low) in enumerate(
        zip(gets, (mine, theirs, mine, theirs), (640, 640, 0, 0))
    ):
        on = make(52 + i, strip(start, low, 128), strip(start, low, 128), sibling)
        halo_kept.append((flag, on))

        @pl.when(flag)
        def _():
            halo[i].wait_recv()
            on.start()
    far.wait_recv()
    far_on = pass_on(56, strip(theirs, 128, 512))
    cut.wait_recv()
    around = []
    for i, target in enumerate(along_y):
        copy = make(48 + i, plane(other, y), plane(other, y), target)
        copy.start()
        around.append(copy)
    planes_on = [pass_on(51, plane(other, y))]
    near.wait_recv()
    far_on.wait_recv()
    for flag, on in halo_kept:
        pl.when(flag)(on.wait_recv)

    light[...] = jnp.zeros_like(light)
    factor[0] = jnp.zeros((N, N), f32)

    def picks(height, width, shift, down):
        high = lax.broadcasted_iota(jnp.int32, (height, width), 0)
        wide = lax.broadcasted_iota(jnp.int32, (height, width), 1)
        hit = high == wide + shift if down else wide == high + shift
        return jnp.where(hit, 1.0, 0.0).astype(bf)

    def scatter(c):
        spread_rows = [
            dot(picks(512, N, rows[s], True), terms[s]).astype(bf) for s in range(slots)
        ]
        for s in range(slots):
            to_cols[s * N:(s + 1) * N, :] = picks(N, 768, cols[s], False)
        total[c] = dot(jnp.concatenate(spread_rows, 1), to_cols[...])

    for s in range(slots):
        from_cols = picks(768, N, cols[s], True)
        from_rows = picks(N, 512, rows[s], False)
        for c in range(2):
            narrow = dot(ext[c], from_cols).astype(bf)
            patch[s, c] = dot(from_rows, narrow)
        factor[0] += patch[s, 0] * patch[s, 0] + patch[s, 1] * patch[s, 1]
    out_power[...] = factor[0].astype(bf)
    power_copy = make(0, out_power, got_power, sibling)
    power_copy.start()

    def sibling_rows(c, out, k):
        for h in range(2):
            start = pl.multiple_of((2 * h + 1 - core) * 128, 128)
            out[h, k] = total[c, pl.ds(start, 128), :].astype(bf)

    def own_rows(c, h, got, k):
        start = pl.multiple_of((2 * h + core) * 128, 128)
        return total[c, pl.ds(start, 128), :] + got[h, k].astype(f32)

    def fan_out(first, far, far_got, halo, halo_got):
        copies = [
            make(first, far.at[:, :, pl.ds(128, 512)], far_got, opposite),
            make(first + 1, halo.at[0], halo_got.at[0], halo_to[0]),
            make(first + 2, far.at[:, :, pl.ds(0, 128)], halo_got.at[1], halo_to[1]),
            make(first + 3, halo.at[1], halo_got.at[2], halo_to[2]),
            make(first + 4, far.at[:, :, pl.ds(640, 128)], halo_got.at[3], halo_to[3]),
        ]
        for copy in copies:
            copy.start()
        return copies

    keep_left = jnp.where(tile > 0, 1.0, 0.0)
    keep_right = jnp.where(tile < tiles - 1, 1.0, 0.0)

    def merged(kept, far_got, halo_got, k):
        center = kept[:, 128:640] + far_got[k].astype(f32)
        from_right = (halo_got[0, k].astype(f32) + halo_got[1, k].astype(f32)) * keep_right
        from_left = (halo_got[2, k].astype(f32) + halo_got[3, k].astype(f32)) * keep_left
        return jnp.concatenate(
            [center[:, :128] + from_left, center[:, 128:384], center[:, 384:] + from_right], 1
        )

    for i, step in enumerate((1, 3, 2)):
        around[i].wait_recv()
        planes_on.append(pass_on(57 + i, plane(other, (y + Y - step) % Y)))
    loads[2].wait()
    loads[3].wait()
    powers[...] = jnp.zeros_like(powers)

    def spectra(q, _):
        g = jnp.where(q % 2 == 0, group, group + 1 - 2 * core)
        g = jnp.where(q < 2, g, (g + 2) % 4)

        @pl.when(q == 1)
        def _():
            own.wait_recv()

        @pl.when(q == 3)
        def _():
            for copy in planes_on:
                copy.wait_recv()

        for s in range(slots):
            ar = patch[s, 0]
            ai = patch[s, 1]
            for k in range(2):
                pr = modes[g, 2 * k].astype(f32)
                pi = modes[g, 2 * k + 1].astype(f32)
                wave = jnp.concatenate([pr * ar - pi * ai, pr * ai + pi * ar], 1).astype(bf)
                half = dot(wave, fwd[...]).astype(bf)
                spectrum = dot(inv[...], jnp.concatenate([half[:, :N], half[:, N:]], 0))
                spec[s, 2 * g + k] = spectrum
                powers[s] += spectrum[:N] * spectrum[:N] + spectrum[N:] * spectrum[N:]
        return 0
    lax.fori_loop(0, 4, spectra, 0)
    loads[4].wait()
    for s in range(slots):
        factor[s] = meas[s] * lax.rsqrt(jnp.maximum(powers[s], 0.25)) - 1.0

    def mode_light(g, _):
        for k in range(2):
            re = modes[g, 2 * k].astype(f32)
            im = modes[g, 2 * k + 1].astype(f32)
            light[...] += re * re + im * im
        return 0
    lax.fori_loop(0, 4, mode_light, 0)

    for s in range(slots):
        terms[s] = light[...].astype(bf)
    scatter(0)
    sibling_rows(0, out_light, 0)
    light_copy = make(1, out_light, got_light, sibling)
    light_copy.start()
    grads[...] = jnp.zeros_like(grads)

    def passed(q):
        return make(7 + q, out_probe.at[q], got_probe.at[q], sibling)

    def piece(h, xl, j):
        i = (2 * h + xl - x + X) % X
        k = i * Y + j
        start = pl.multiple_of(xl * 128 + ((y + j) % Y) * 32, 32)
        copy = make(
            9 + k, pieces.at[h, :, pl.ds(start, 32), :], got_piece.at[k],
            device(2 * h + xl, (y + j) % Y, z, core),
        )
        return copy, k

    def back_step(q, _):
        h = q % 2
        side = jnp.where(q < 2, 1 - core, core)
        g = 2 * h + side
        sums[...] = jnp.zeros_like(sums)
        for s in range(slots):
            fac = factor[s]
            ar = patch[s, 0]
            ai = patch[s, 1]
            for k in range(2):
                spectrum = spec[s, 2 * g + k]
                diff = jnp.concatenate([spectrum[:N] * fac, spectrum[N:] * fac], 0).astype(bf)
                half = dot(fwd[...], diff).astype(bf)
                back = dot(jnp.concatenate([half[:N], half[N:]], 1), inv[...])
                br = back[:, :N]
                bi = back[:, N:]
                pr = modes[g, 2 * k].astype(f32)
                pi = modes[g, 2 * k + 1].astype(f32)
                sums[2 * k] += ar * br + ai * bi
                sums[2 * k + 1] += ar * bi - ai * br
                grads[s, 0] += pr * br + pi * bi
                grads[s, 1] += pr * bi - pi * br

        @pl.when(q < 2)
        def _():
            out_probe[h] = sums[...].astype(bf)
            passed(h).start()

        @pl.when(q >= 2)
        def _():
            passed(h).wait_recv()
            for k in range(4):
                pieces[h, k] = (sums[k] + got_probe[h, k].astype(f32)).astype(bf)
            for xl in range(2):
                for j in range(Y):
                    copy, k = piece(h, xl, j)
                    if j:
                        copy.start()
                    else:
                        pl.when(k > 0)(copy.start)
        return 0
    lax.fori_loop(0, 1, back_step, 0)
    light_copy.wait_recv()
    kept_light = own_rows(0, x_hi, got_light, 0)
    far_light[0] = own_rows(0, 1 - x_hi, got_light, 0).astype(bf)
    halo_light[0, 0] = kept_light[:, :128].astype(bf)
    halo_light[1, 0] = kept_light[:, 640:].astype(bf)
    light_copies = fan_out(2, far_light, far_got_light, halo_light, halo_got_light)
    power_copy.wait_recv()
    total_power = (out_power[...].astype(f32) + got_power[...].astype(f32)).astype(bf)
    pieces[0, 4] = total_power
    pieces[1, 4] = total_power

    lax.fori_loop(1, 4, back_step, 0)

    for copy in light_copies:
        copy.wait_recv()
    weight = merged(kept_light, far_got_light, halo_got_light, 0) + object_reg

    for c in range(2):
        for s in range(slots):
            terms[s] = grads[s, c].astype(bf)
        scatter(c)
    for c in range(2):
        sibling_rows(c, out_grad, c)
    grad_copy = make(32, out_grad, got_grad, sibling)
    grad_copy.start()

    band_start = pl.multiple_of((x % 2) * 128 + y * 32, 32)
    band = pieces[x_hi, :, pl.ds(band_start, 32), :].astype(f32)
    grad_copy.wait_recv()
    for c in range(2):
        far_grad[c] = own_rows(c, 1 - x_hi, got_grad, c).astype(bf)
        halo_grad[0, c] = own_rows(c, x_hi, got_grad, c)[:, :128].astype(bf)
        halo_grad[1, c] = own_rows(c, x_hi, got_grad, c)[:, 640:].astype(bf)
    grad_copies = fan_out(33, far_grad, far_got_grad, halo_grad, halo_got_grad)

    def arrived(k):
        return make(9 + k, pieces.at[0, :, pl.ds(0, 32), :], got_piece.at[k], sibling)
    for k in range(1, X * Y):
        arrived(k).wait_recv()
        band = band + got_piece[k].astype(f32)
    for part in range(Z):
        for k in range(5):
            bands[part, 4 * k:4 * k + 4] = band[k, 4 * part:4 * part + 4]
    band_copies = []
    for i in range(1, Z):
        copy = make(24 + i, bands.at[(z + i) % Z], got_band.at[i - 1], along_z[i - 1])
        copy.start()
        band_copies.append(copy)

    for copy in grad_copies:
        copy.wait_recv()
    for c in range(2):
        kept = own_rows(c, x_hi, got_grad, c)
        object_out[c] = obj[c] + merged(kept, far_got_grad, halo_got_grad, c) / weight

    final = bands[z]
    for i in range(Z - 1):
        band_copies[i].wait_recv()
        final = final + got_band[i]
    weight = final[16:20] + probe_reg
    at = pl.multiple_of((tile // 2) * 8, 8)
    for k in range(4):
        rows8 = probe[k // 2, k % 2, pl.ds(at, 8), :]
        probe_row = jnp.where(tile % 2 == 0, rows8[:4], rows8[4:])
        probe_out[k] = probe_row + final[4 * k:4 * k + 4] / weight
    for copy in [far, cut, near, own, far_on] + around + planes_on:
        copy.wait_send()
    for flag, copy in zip(sends, halo):
        pl.when(flag)(copy.wait_send)
    for flag, copy in halo_kept:
        pl.when(flag)(copy.wait_send)
    for copy in [power_copy, light_copy, grad_copy, passed(0), passed(1)] + light_copies + grad_copies + band_copies:
        copy.wait_send()
    for k in range(1, X * Y):
        arrived(k).wait_send()


def refine(counts, rows, cols, obj, probe, meas):
    forward, inverse = tables()
    whole = pl.BlockSpec(memory_space=pltpu.VMEM)
    scalars = pl.BlockSpec(memory_space=pltpu.SMEM)
    remote = pl.BlockSpec(memory_space=pl.ANY)
    return pl.pallas_call(
        refine_kernel,
        out_shape=(
            jax.ShapeDtypeStruct((2, 128, 512), f32), jax.ShapeDtypeStruct((4, 4, N), f32)
        ),
        in_specs=[scalars] * 3 + [remote] * 5,
        out_specs=(whole, whole),
        scratch_shapes=[
            pltpu.VMEM((2, 128, 512), f32),
            pltpu.VMEM((2, 2, N, N), f32),
            pltpu.VMEM((3, N, N), f32),
            pltpu.VMEM((2 * N, 2 * N), bf),
            pltpu.VMEM((2 * N, 2 * N), bf),
            pltpu.VMEM((2, 128, 512), bf),
            pltpu.VMEM((2, 512, 768), bf),
            pltpu.VMEM((4, 4, N, N), bf),
            pltpu.VMEM((3, N, N), f32),
            pltpu.VMEM((3, 2, N, N), f32),
            pltpu.VMEM((3, N, N), f32),
            pltpu.VMEM((3, 8, 2 * N, N), f32),
            pltpu.VMEM((N, N), f32),
            pltpu.VMEM((3, N, N), bf),
            pltpu.VMEM((3 * N, 768), bf),
            pltpu.VMEM((2, 512, 768), f32),
            pltpu.VMEM((3, 2, N, N), f32),
            pltpu.VMEM((4, N, N), f32),
            pltpu.VMEM((2, 4, N, N), bf),
            pltpu.VMEM((2, 4, N, N), bf),
            pltpu.VMEM((N, N), bf),
            pltpu.VMEM((N, N), bf),
            pltpu.VMEM((2, 5, N, N), bf),
            pltpu.VMEM((X * Y, 5, 32, N), bf),
            pltpu.VMEM((Z, 24, N), f32),
            pltpu.VMEM((Z - 1, 24, N), f32),
            pltpu.VMEM((2, 1, 128, 768), bf),
            pltpu.VMEM((2, 1, 128, 768), bf),
            pltpu.VMEM((1, 128, 768), bf),
            pltpu.VMEM((1, 128, 512), bf),
            pltpu.VMEM((2, 1, 128, 128), bf),
            pltpu.VMEM((4, 1, 128, 128), bf),
            pltpu.VMEM((2, 2, 128, 768), bf),
            pltpu.VMEM((2, 2, 128, 768), bf),
            pltpu.VMEM((2, 128, 768), bf),
            pltpu.VMEM((2, 128, 512), bf),
            pltpu.VMEM((2, 2, 128, 128), bf),
            pltpu.VMEM((4, 2, 128, 128), bf),
            pltpu.SemaphoreType.DMA((60,)), pltpu.SemaphoreType.DMA((60,)),
            pltpu.SemaphoreType.DMA((5,)),
        ],
        compiler_params=pltpu.CompilerParams(
            collective_id=1, has_side_effects=True, vmem_limit_bytes=60 * 2**20
        ),
        name="refine",
    )(counts, rows, cols, obj, probe, meas, jnp.asarray(forward), jnp.asarray(inverse))


def local(object_field, probe, measured, scan_rows, scan_cols, counts):
    object_out, probe_out = refine(counts, scan_rows, scan_cols, object_field, probe, measured)
    return object_out, probe_out.reshape(2, 2, 4, N)


def solution(mesh):
    return jax.shard_map(
        local,
        mesh=mesh,
        in_specs=(
            P(None, "mode", "tile"),
            P("mode", None, None, None),
            P(("tile", "mode"), None, None),
            P(("tile", "mode")),
            P(("tile", "mode")),
            P("tile"),
        ),
        out_specs=(P(None, "mode", "tile"), P("mode", None, "tile", None)),
        check_vma=False,
    )
```

```python
import functools

import jax
import jax.numpy as jnp
import ml_dtypes
import numpy as np
from jax import lax
from jax.experimental import pallas as pl
from jax.experimental.pallas import tpu as pltpu
from jax.sharding import PartitionSpec as P

object_reg = 0.5
probe_reg = 1.0
N = 256
H = N // 2
X, Y, Z = 4, 4, 8
bf = jnp.bfloat16
f32 = jnp.float32
MESH = pl.DeviceIdType.MESH


def tables():
    pos = np.arange(N)
    ang = (pos[:, None] * pos[None, :] % N) * (2.0 * np.pi / N)
    sc = 1.0 / np.sqrt(float(N))
    re = (np.cos(ang) * sc).astype(ml_dtypes.bfloat16)
    im = (-np.sin(ang) * sc).astype(ml_dtypes.bfloat16)
    out = []
    for p in range(2):
        c, s = re[:H, p::2], im[:H, p::2]
        out.append(np.block([[c, s], [-s, c]]))
    for p in range(2):
        c, s = re[p::2, :H], im[p::2, :H]
        out.append(np.block([[c, -s], [s, c]]))
    for p in range(2):
        c, s = re[:H, p::2], im[:H, p::2]
        out.append(np.block([[c, s], [-s, c]]))
    for p in range(2):
        c, s = re[p::2, :H], im[p::2, :H]
        out.append(np.block([[c, -s], [s, c]]))
    return np.stack(out).astype(ml_dtypes.bfloat16)


def side(parts):
    return jnp.concatenate(parts, 1)


def stack(parts):
    return jnp.concatenate(parts, 0)


def dot(a, b):
    return jnp.dot(a, b, preferred_element_type=f32)


def here():
    tile = lax.axis_index("tile")
    group = lax.axis_index("mode")
    x = (group // 2) * 2 + tile // (Y * Z)
    return tile, group, x, (tile // Z) % Y, tile % Z, group % 2


def device(x, y, z, core):
    return {"tile": (x % 2) * (Y * Z) + y * Z + z, "mode": (x // 2) * 2 + core}


def sender(send_sem, recv_sem):
    def make(index, src, dst, target):
        return pltpu.make_async_remote_copy(
            src_ref=src, dst_ref=dst, send_sem=send_sem.at[index], recv_sem=recv_sem.at[index],
            device_id=target, device_id_type=MESH,
        )
    return make


def refine_kernel(counts, rows_in, cols, obj_in, probe_in, meas_in, dft_in, object_out, probe_out,
                  obj, probe, meas, dft, block, ext, modes, powers,
                  from_cols, from_rows, to_rows, narrow, by, kept_light,
                  patch, factor, spec, light, terms, to_cols, total, grads,
                  out_probe, got_probe, out_power, got_power, pieces, got_y, whole_power, got_power_y,
                  wide, bands, got_z, rims, got_x, last_power, got_power_x,
                  out_light, got_light, far_light, far_got_light, halo_light, halo_got_light,
                  out_grad, got_grad, far_grad, far_got_grad, halo_grad, halo_got_grad,
                  send_sem, recv_sem, load_sem):
    loads = [
        pltpu.make_async_copy(src, dst, load_sem.at[i])
        for i, (src, dst) in enumerate(
            ((obj_in, obj), (probe_in, probe), (meas_in, meas), (dft_in, dft))
        )
    ]
    for load in loads:
        load.start()
    slots = 3
    tile, group, x, y, z, core = here()
    tiles = X * Y * Z // 2
    x_hi = group // 2
    sibling = device(x, y, z, 1 - core)
    opposite = device((x + 2) % X, y, z, core)
    before, after = (tile + tiles - 1) % tiles, (tile + 1) % tiles
    other = (group + 2) % 4
    halo_to = [
        {"tile": before, "mode": group}, {"tile": before, "mode": other},
        {"tile": after, "mode": group}, {"tile": after, "mode": other},
    ]
    along_x = [device((x + i) % X, y, z, core) for i in (1, 3, 2)]
    along_z = [device(x, y, (z + i) % Z, core) for i in range(1, Z)]
    make = sender(send_sem, recv_sem)

    across = device(X - 1 - x, y, z, core)
    along_y = [device(x, (y + i) % Y, z, core) for i in (1, 3, 2)]
    partners = [sibling] + halo_to + along_x + along_y + along_z
    barrier = pltpu.get_barrier_semaphore()
    for partner in partners:
        pl.semaphore_signal(barrier, inc=1, device_id=partner, device_id_type=MESH)
    rows = [jnp.where(group * slots + s < counts[0], rows_in[s], 4096) for s in range(slots)]

    mine = pl.multiple_of(group * 128, 128)
    theirs = pl.multiple_of(other * 128, 128)
    loads[0].wait()
    block[...] = obj[...].astype(bf)
    ext[:, pl.ds(mine, 128), 128:640] = block[...]

    @pl.when(tile == 0)
    def _():
        ext[:, :, :128] = jnp.zeros((2, 512, 128), bf)

    @pl.when(tile == tiles - 1)
    def _():
        ext[:, :, 640:] = jnp.zeros((2, 512, 128), bf)

    loads[1].wait()
    for k in range(2):
        for c in range(2):
            modes[group, 2 * k + c] = probe[k, c].astype(bf)
    pl.semaphore_wait(barrier, len(partners))

    def strip(start, low, width):
        return ext.at[:, pl.ds(start, 128), pl.ds(low, width)]

    def plane(which, index):
        return modes.at[which, pl.ds(index, 1)]

    cut = make(41, plane(group, y), plane(group, y), across)
    cut.start()
    own = make(47, modes.at[group], modes.at[group], sibling)
    own.start()
    far = make(40, block, strip(mine, 128, 512), opposite)
    far.start()
    left, right = block.at[:, :, pl.ds(0, 128)], block.at[:, :, pl.ds(384, 128)]
    halo = [
        make(42, left, strip(mine, 640, 128), halo_to[0]),
        make(43, left, strip(mine, 640, 128), halo_to[1]),
        make(44, right, strip(mine, 0, 128), halo_to[2]),
        make(45, right, strip(mine, 0, 128), halo_to[3]),
    ]
    sends = (tile > 0, tile > 0, tile < tiles - 1, tile < tiles - 1)
    gets = (tile < tiles - 1, tile < tiles - 1, tile > 0, tile > 0)
    for flag, copy in zip(sends, halo):
        pl.when(flag)(copy.start)
    near = make(46, block, strip(mine, 128, 512), sibling)
    near.start()

    def pass_on(index, ref):
        copy = make(index, ref, ref, sibling)
        copy.start()
        return copy

    def picks(height, width, shift, down):
        high = lax.broadcasted_iota(jnp.int32, (height, width), 0)
        wide = lax.broadcasted_iota(jnp.int32, (height, width), 1)
        hit = high == wide + shift if down else wide == high + shift
        return jnp.where(hit, 1.0, 0.0).astype(bf)

    def sorted_by_parity(down):
        high = lax.broadcasted_iota(jnp.int32, (N, N), 0)
        wide = lax.broadcasted_iota(jnp.int32, (N, N), 1)
        place, held = (high, wide) if down else (wide, high)
        hit = held == jnp.where(place < N // 2, 2 * place, 2 * place - (N - 1))
        return jnp.where(hit, 1.0, 0.0).astype(f32)

    for s in range(slots):
        from_cols[s] = picks(768, N, cols[s], True)
        from_rows[s] = picks(N, 512, rows[s], False)
        to_rows[s] = picks(512, N, rows[s], True)
        to_cols[s * N:(s + 1) * N, :] = picks(N, 768, cols[s], False)
    light[...] = jnp.zeros_like(light)
    wide[...] = jnp.zeros_like(wide)
    powers[...] = jnp.zeros_like(powers)
    grads[...] = jnp.zeros_like(grads)
    loads[2].wait()
    for s in range(slots):
        by_cols = jnp.dot(meas[s], sorted_by_parity(False), precision=lax.Precision.HIGHEST,
                          preferred_element_type=f32)
        meas[s] = jnp.dot(sorted_by_parity(True), by_cols, precision=lax.Precision.HIGHEST,
                          preferred_element_type=f32)

    def scatter(c):
        spread_rows = [dot(to_rows[s], terms[s]).astype(bf) for s in range(slots)]
        total[c] = dot(jnp.concatenate(spread_rows, 1), to_cols[...])

    def sibling_rows(c, out, k):
        for h in range(2):
            start = pl.multiple_of((2 * h + 1 - core) * 128, 128)
            out[h, k] = total[c, pl.ds(start, 128), :].astype(bf)

    def own_rows(c, h, got, k):
        start = pl.multiple_of((2 * h + core) * 128, 128)
        return total[c, pl.ds(start, 128), :] + got[h, k].astype(f32)

    def fan_out(first, far, far_got, halo, halo_got):
        copies = [
            make(first, far.at[:, :, pl.ds(128, 512)], far_got, opposite),
            make(first + 1, halo.at[0], halo_got.at[0], halo_to[0]),
            make(first + 2, far.at[:, :, pl.ds(0, 128)], halo_got.at[1], halo_to[1]),
            make(first + 3, halo.at[1], halo_got.at[2], halo_to[2]),
            make(first + 4, far.at[:, :, pl.ds(640, 128)], halo_got.at[3], halo_to[3]),
        ]
        for copy in copies:
            copy.start()
        return copies

    keep_left = jnp.where(tile > 0, 1.0, 0.0)
    keep_right = jnp.where(tile < tiles - 1, 1.0, 0.0)

    def merged(kept, far_got, halo_got, k):
        center = kept[:, 128:640] + far_got[k].astype(f32)
        from_right = (halo_got[0, k].astype(f32) + halo_got[1, k].astype(f32)) * keep_right
        from_left = (halo_got[2, k].astype(f32) + halo_got[3, k].astype(f32)) * keep_left
        return jnp.concatenate(
            [center[:, :128] + from_left, center[:, 128:384], center[:, 384:] + from_right], 1
        )

    cut.wait_recv()
    around = []
    for i, target in enumerate(along_y):
        copy = make(48 + i, plane(other, y), plane(other, y), target)
        copy.start()
        around.append(copy)
    planes_on = [pass_on(51, plane(other, y))]

    def narrow_rows(which):
        start = pl.multiple_of(which * 128, 128)
        for s in range(slots):
            for c in range(2):
                narrow[s, c, pl.ds(start, 128), :] = dot(
                    ext[c, pl.ds(start, 128), :], from_cols[s]
                ).astype(bf)

    halo_kept = []
    for i, (flag, start, low) in enumerate(
        zip(gets, (mine, theirs, mine, theirs), (640, 640, 0, 0))
    ):
        halo_kept.append((flag, make(52 + i, strip(start, low, 128), strip(start, low, 128), sibling)))

    def halo_on(i):
        flag, on = halo_kept[i]

        @pl.when(flag)
        def _():
            halo[i].wait_recv()
            on.start()

    def halo_in(i):
        flag, on = halo_kept[i]
        pl.when(flag)(on.wait_recv)

    halo_on(0)
    halo_on(2)
    narrow_rows(group)
    near.wait_recv()
    halo_in(0)
    halo_in(2)
    narrow_rows(group + 1 - 2 * core)
    for i, step in enumerate((1, 3, 2)):
        around[i].wait_recv()
        planes_on.append(pass_on(57 + i, plane(other, (y + Y - step) % Y)))
    halo_on(1)
    halo_on(3)
    far.wait_recv()
    far_on = pass_on(56, strip(theirs, 128, 512))
    narrow_rows(other)
    own.wait_recv()
    for copy in planes_on:
        copy.wait_recv()
    def mode_light(g, _):
        for k in range(2):
            re = modes[g, 2 * k].astype(f32)
            im = modes[g, 2 * k + 1].astype(f32)
            light[...] += re * re + im * im
        return 0
    lax.fori_loop(0, 4, mode_light, 0)

    for s in range(slots):
        terms[s] = light[...].astype(bf)
    scatter(0)
    sibling_rows(0, out_light, 0)
    light_copy = make(1, out_light, got_light, sibling)
    light_copy.start()
    far_on.wait_recv()
    halo_in(1)
    halo_in(3)
    narrow_rows((other // 2) * 2 + 1 - core)
    for s in range(slots):
        for c in range(2):
            patch[s, c] = dot(from_rows[s], narrow[s, c])
    factor[0] = patch[0, 0] * patch[0, 0] + patch[0, 1] * patch[0, 1]
    for s in range(1, slots):
        factor[0] += patch[s, 0] * patch[s, 0] + patch[s, 1] * patch[s, 1]
    out_power[...] = factor[0].astype(bf)
    power_copy = make(0, out_power, got_power, sibling)
    power_copy.start()
    loads[3].wait()
    light_copy.wait_recv()
    kept = own_rows(0, x_hi, got_light, 0)
    kept_light[...] = kept
    far_light[0] = own_rows(0, 1 - x_hi, got_light, 0).astype(bf)
    halo_light[0, 0] = kept[:, :128].astype(bf)
    halo_light[1, 0] = kept[:, 640:].astype(bf)
    light_copies = fan_out(2, far_light, far_got_light, halo_light, halo_got_light)

    def spectra(m, _):
        pr = modes[m // 2, 2 * (m % 2)].astype(f32)
        pi = modes[m // 2, 2 * (m % 2) + 1].astype(f32)
        added, taken = [], []
        for s in range(slots):
            re = pr * patch[s, 0] - pi * patch[s, 1]
            im = pr * patch[s, 1] + pi * patch[s, 0]
            added.append(side([re[:, :H] + re[:, H:], im[:, :H] + im[:, H:]]).astype(bf))
            taken.append(side([re[:, :H] - re[:, H:], im[:, :H] - im[:, H:]]).astype(bf))
        even = dot(stack(added), dft[0])
        odd = dot(stack(taken), dft[1])
        added, taken = [], []
        for s in range(slots):
            low, high = slice(s * N, s * N + H), slice(s * N + H, (s + 1) * N)
            e, o = even[low] + even[high], odd[low] + odd[high]
            added.append(stack([side([e[:, :H], o[:, :H]]), side([e[:, H:], o[:, H:]])]).astype(bf))
            e, o = even[low] - even[high], odd[low] - odd[high]
            taken.append(stack([side([e[:, :H], o[:, :H]]), side([e[:, H:], o[:, H:]])]).astype(bf))
        even = dot(dft[2], side(added))
        odd = dot(dft[3], side(taken))
        spec[m, :N] = even
        spec[m, N:] = odd
        for s in range(slots):
            e, o = even[:, s * N:(s + 1) * N], odd[:, s * N:(s + 1) * N]
            powers[s, :H] += e[:H] * e[:H] + e[H:] * e[H:]
            powers[s, H:] += o[:H] * o[:H] + o[H:] * o[H:]
        return 0
    lax.fori_loop(0, 8, spectra, 0, unroll=2)
    for s in range(slots):
        ratio = meas[s] * lax.rsqrt(jnp.maximum(powers[s], 0.25)) - 1.0
        for p in range(2):
            rows_p = ratio[p * H:(p + 1) * H]
            by[p, :, s * N:(s + 1) * N] = stack([rows_p, rows_p])


    def passed(i):
        return make(60 + i, out_probe.at[i], got_probe.at[i], sibling)

    def to_y(i, j):
        k = 3 * i + j - 1
        return make(70 + k, pieces.at[i, :, :, (y + j) % Y], got_y.at[k], device(x, (y + j) % Y, z, core))

    def power_y(j):
        return make(82 + j, whole_power.at[:, (y + j) % Y], got_power_y.at[j - 1],
                    device(x, (y + j) % Y, z, core))

    def to_z(h, i):
        height = 48 if h == 0 else 32
        return make(
            86 + 8 * h + i, bands.at[h, (z + i) % Z, pl.ds(0, height)],
            got_z.at[h, i, pl.ds(0, height)], along_z[i - 1]
        )

    def to_x(h, xl):
        i = (2 * h + xl - x + X) % X
        return make(104 + i, rims.at[h, pl.ds(16 * xl, 16)], got_x.at[i], device(2 * h + xl, y, z, core)), i

    def power_x(i):
        return make(108 + i, last_power.at[(x + i) % 2], got_power_x.at[i], device((x + i) % X, y, z, core))

    def reduce_y(h):
        for p in range(2):
            i = 2 * h + p
            band = pieces[i, :, :, y].astype(f32)
            for j in range(1, Y):
                to_y(i, j).wait_recv()
                band = band + got_y[3 * i + j - 1].astype(f32)
            for part in range(Z):
                for xl in range(2):
                    for c in range(2):
                        at = 16 * xl + 8 * p + 4 * c
                        wide[part, at:at + 4] = band[c, xl, 4 * part:4 * part + 4]
        if h == 0:
            band = whole_power[:, y].astype(f32)
            for j in range(1, Y):
                power_y(j).wait_recv()
                band = band + got_power_y[j - 1].astype(f32)
            for part in range(Z):
                for xl in range(2):
                    wide[part, 32 + 4 * xl:36 + 4 * xl] = band[xl, 4 * part:4 * part + 4]
        bands[h] = wide[...].astype(bf)
        for i in range(1, Z):
            to_z(h, i).start()

    def reduce_z(h):
        height = 48 if h == 0 else 32
        total_z = bands[h, z, :height].astype(f32)
        for i in range(1, Z):
            to_z(h, i).wait_recv()
            total_z = total_z + got_z[h, i, :height].astype(f32)
        rims[h] = total_z[:32]
        for xl in range(2):
            copy, i = to_x(h, xl)
            pl.when(i > 0)(copy.start)
        if h == 0:
            for xl in range(2):
                last_power[xl, :4] = total_z[32 + 4 * xl:36 + 4 * xl]
                last_power[xl, 4:] = total_z[36:40]
            for i in range(1, X):
                power_x(i).start()

    def back_step(step, _):
        i = step // 2
        m = 4 * (i // 2) + 2 * jnp.where(step % 2 == 0, 1 - core, core) + i % 2
        pr = modes[m // 2, 2 * (m % 2)].astype(f32)
        pi = modes[m // 2, 2 * (m % 2) + 1].astype(f32)
        even = dot(dft[4], (spec[m, :N] * by[0]).astype(bf))
        odd = dot(dft[5], (spec[m, N:] * by[1]).astype(bf))
        low, high = (even + odd).astype(bf), (even - odd).astype(bf)
        at_even, at_odd = [], []
        for s in range(slots):
            c, d = slice(s * N, s * N + H), slice(s * N + H, (s + 1) * N)
            at_even.append(side([stack([low[:H, c], high[:H, c]]), stack([low[H:, c], high[H:, c]])]))
            at_odd.append(side([stack([low[:H, d], high[:H, d]]), stack([low[H:, d], high[H:, d]])]))
        even = dot(stack(at_even), dft[6])
        odd = dot(stack(at_odd), dft[7])
        low, high = even + odd, even - odd
        sum_re, sum_im = None, None
        for s in range(slots):
            r = slice(s * N, (s + 1) * N)
            br = side([low[r, :H], high[r, :H]])
            bi = side([low[r, H:], high[r, H:]])
            ar = patch[s, 0]
            ai = patch[s, 1]
            re = ar * br + ai * bi
            im = ar * bi - ai * br
            sum_re = re if s == 0 else sum_re + re
            sum_im = im if s == 0 else sum_im + im
            grads[s, 0] += pr * br + pi * bi
            grads[s, 1] += pr * bi - pi * br

        @pl.when(step % 2 == 0)
        def _():
            out_probe[i, 0] = sum_re.astype(bf)
            out_probe[i, 1] = sum_im.astype(bf)
            passed(i).start()

        @pl.when(step % 2 == 1)
        def _():
            passed(i).wait_recv()
            for c, mine_sum in enumerate((sum_re, sum_im)):
                both = (mine_sum + got_probe[i, c].astype(f32)).astype(bf)
                pieces[i, c] = both.reshape(2, Y, 32, N)
            for j in range(1, Y):
                to_y(i, j).start()
        return 0

    power_copy.wait_recv()
    whole_power[...] = (out_power[...].astype(f32) + got_power[...].astype(f32)).astype(bf).reshape(2, Y, 32, N)
    for j in range(1, Y):
        power_y(j).start()
    lax.fori_loop(0, 8, back_step, 0)

    for copy in light_copies:
        copy.wait_recv()
    weight = merged(kept_light[...], far_got_light, halo_got_light, 0) + object_reg

    for c in range(2):
        for s in range(slots):
            terms[s] = grads[s, c].astype(bf)
        scatter(c)
    for c in range(2):
        sibling_rows(c, out_grad, c)
    grad_copy = make(32, out_grad, got_grad, sibling)
    grad_copy.start()
    reduce_y(0)
    grad_copy.wait_recv()
    for c in range(2):
        far_grad[c] = own_rows(c, 1 - x_hi, got_grad, c).astype(bf)
        halo_grad[0, c] = own_rows(c, x_hi, got_grad, c)[:, :128].astype(bf)
        halo_grad[1, c] = own_rows(c, x_hi, got_grad, c)[:, 640:].astype(bf)
    grad_copies = fan_out(33, far_grad, far_got_grad, halo_grad, halo_got_grad)

    reduce_y(1)
    reduce_z(0)
    reduce_z(1)
    for copy in grad_copies:
        copy.wait_recv()
    for c in range(2):
        kept = own_rows(c, x_hi, got_grad, c)
        object_out[c] = obj[c] + merged(kept, far_got_grad, halo_got_grad, c) / weight

    final = rims[x_hi, pl.ds(pl.multiple_of(16 * (x % 2), 16), 16)]
    weight = last_power[x % 2, :4] + probe_reg
    for i in range(1, X):
        make(104 + i, rims.at[0, pl.ds(0, 16)], got_x.at[i], sibling).wait_recv()
        final = final + got_x[i]
        power_x(i).wait_recv()
        weight = weight + got_power_x[i, :4]
    at = pl.multiple_of((tile // 2) * 8, 8)
    for k in range(4):
        rows8 = probe[k // 2, k % 2, pl.ds(at, 8), :]
        probe_row = jnp.where(tile % 2 == 0, rows8[:4], rows8[4:])
        probe_out[k] = probe_row + final[4 * k:4 * k + 4] / weight
    for copy in [far, cut, near, own, far_on] + around + planes_on:
        copy.wait_send()
    for flag, copy in zip(sends, halo):
        pl.when(flag)(copy.wait_send)
    for flag, copy in halo_kept:
        pl.when(flag)(copy.wait_send)
    for copy in [power_copy, light_copy, grad_copy, ] + light_copies + grad_copies:
        copy.wait_send()
    for i in range(4):
        passed(i).wait_send()
        for j in range(1, Y):
            to_y(i, j).wait_send()
    for h in range(2):
        for i in range(1, Z):
            to_z(h, i).wait_send()
    for j in range(1, Y):
        power_y(j).wait_send()
    for i in range(1, X):
        make(104 + i, rims.at[0, pl.ds(0, 16)], got_x.at[i], sibling).wait_send()
        power_x(i).wait_send()


def refine(counts, rows, cols, obj, probe, meas):
    whole = pl.BlockSpec(memory_space=pltpu.VMEM)
    scalars = pl.BlockSpec(memory_space=pltpu.SMEM)
    remote = pl.BlockSpec(memory_space=pl.ANY)
    return pl.pallas_call(
        refine_kernel,
        out_shape=(
            jax.ShapeDtypeStruct((2, 128, 512), f32), jax.ShapeDtypeStruct((4, 4, N), f32)
        ),
        in_specs=[scalars] * 3 + [remote] * 4,
        out_specs=(whole, whole),
        scratch_shapes=[
            pltpu.VMEM((2, 128, 512), f32),
            pltpu.VMEM((2, 2, N, N), f32),
            pltpu.VMEM((3, N, N), f32),
            pltpu.VMEM((8, N, N), bf),
            pltpu.VMEM((2, 128, 512), bf),
            pltpu.VMEM((2, 512, 768), bf),
            pltpu.VMEM((4, 4, N, N), bf),
            pltpu.VMEM((3, N, N), f32),
            pltpu.VMEM((3, 768, N), bf),
            pltpu.VMEM((3, N, 512), bf),
            pltpu.VMEM((3, 512, N), bf),
            pltpu.VMEM((3, 2, 512, N), bf),
            pltpu.VMEM((2, N, 3 * N), f32),
            pltpu.VMEM((128, 768), f32),
            pltpu.VMEM((3, 2, N, N), f32),
            pltpu.VMEM((3, N, N), f32),
            pltpu.VMEM((8, 2 * N, 3 * N), f32),
            pltpu.VMEM((N, N), f32),
            pltpu.VMEM((3, N, N), bf),
            pltpu.VMEM((3 * N, 768), bf),
            pltpu.VMEM((2, 512, 768), f32),
            pltpu.VMEM((3, 2, N, N), f32),
            pltpu.VMEM((4, 2, N, N), bf),
            pltpu.VMEM((4, 2, N, N), bf),
            pltpu.VMEM((N, N), bf),
            pltpu.VMEM((N, N), bf),
            pltpu.VMEM((4, 2, 2, Y, 32, N), bf),
            pltpu.VMEM((12, 2, 2, 32, N), bf),
            pltpu.VMEM((2, Y, 32, N), bf),
            pltpu.VMEM((3, 2, 32, N), bf),
            pltpu.VMEM((Z, 48, N), f32),
            pltpu.VMEM((2, Z, 48, N), bf),
            pltpu.VMEM((2, Z, 48, N), bf),
            pltpu.VMEM((2, 32, N), f32),
            pltpu.VMEM((X, 16, N), f32),
            pltpu.VMEM((2, 8, N), f32),
            pltpu.VMEM((X, 8, N), f32),
            pltpu.VMEM((2, 1, 128, 768), bf),
            pltpu.VMEM((2, 1, 128, 768), bf),
            pltpu.VMEM((1, 128, 768), bf),
            pltpu.VMEM((1, 128, 512), bf),
            pltpu.VMEM((2, 1, 128, 128), bf),
            pltpu.VMEM((4, 1, 128, 128), bf),
            pltpu.VMEM((2, 2, 128, 768), bf),
            pltpu.VMEM((2, 2, 128, 768), bf),
            pltpu.VMEM((2, 128, 768), bf),
            pltpu.VMEM((2, 128, 512), bf),
            pltpu.VMEM((2, 2, 128, 128), bf),
            pltpu.VMEM((4, 2, 128, 128), bf),
            pltpu.SemaphoreType.DMA((112,)), pltpu.SemaphoreType.DMA((112,)),
            pltpu.SemaphoreType.DMA((4,)),
        ],
        compiler_params=pltpu.CompilerParams(
            collective_id=1, has_side_effects=True, vmem_limit_bytes=60 * 2**20
        ),
        name="refine",
    )(counts, rows, cols, obj, probe, meas, jnp.asarray(tables()))


def local(object_field, probe, measured, scan_rows, scan_cols, counts):
    object_out, probe_out = refine(counts, scan_rows, scan_cols, object_field, probe, measured)
    return object_out, probe_out.reshape(2, 2, 4, N)


def solution(mesh):
    return jax.shard_map(
        local,
        mesh=mesh,
        in_specs=(
            P(None, "mode", "tile"),
            P("mode", None, None, None),
            P(("tile", "mode"), None, None),
            P(("tile", "mode")),
            P(("tile", "mode")),
            P("tile"),
        ),
        out_specs=(P(None, "mode", "tile"), P("mode", None, "tile", None)),
        check_vma=False,
    )
```

```python
import functools

import jax
import jax.numpy as jnp
import ml_dtypes
import numpy as np
from jax import lax
from jax.experimental import pallas as pl
from jax.experimental.pallas import tpu as pltpu
from jax.sharding import PartitionSpec as P

object_reg = 0.5
probe_reg = 1.0
N = 256
H = N // 2
X, Y, Z = 4, 4, 8
bf = jnp.bfloat16
f32 = jnp.float32
MESH = pl.DeviceIdType.MESH


def tables():
    pos = np.arange(N)
    ang = (pos[:, None] * pos[None, :] % N) * (2.0 * np.pi / N)
    sc = 1.0 / np.sqrt(float(N))
    re = (np.cos(ang) * sc).astype(ml_dtypes.bfloat16)
    im = (-np.sin(ang) * sc).astype(ml_dtypes.bfloat16)
    out = []
    for p in range(2):
        c, s = re[:H, p::2], im[:H, p::2]
        out.append(np.block([[c, s], [-s, c]]))
    for p in range(2):
        c, s = re[p::2, :H], im[p::2, :H]
        out.append(np.block([[c, -s], [s, c]]))
    for p in range(2):
        c, s = re[:H, p::2], im[:H, p::2]
        out.append(np.block([[c, s], [-s, c]]))
    for p in range(2):
        c, s = re[p::2, :H], im[p::2, :H]
        out.append(np.block([[c, -s], [s, c]]))
    return np.stack(out).astype(ml_dtypes.bfloat16)


def side(parts):
    return jnp.concatenate(parts, 1)


def stack(parts):
    return jnp.concatenate(parts, 0)


def dot(a, b):
    return jnp.dot(a, b, preferred_element_type=f32)


def here():
    tile = lax.axis_index("tile")
    group = lax.axis_index("mode")
    x = (group // 2) * 2 + tile // (Y * Z)
    return tile, group, x, (tile // Z) % Y, tile % Z, group % 2


def device(x, y, z, core):
    return {"tile": (x % 2) * (Y * Z) + y * Z + z, "mode": (x // 2) * 2 + core}


def sender(send_sem, recv_sem):
    def make(index, src, dst, target):
        return pltpu.make_async_remote_copy(
            src_ref=src, dst_ref=dst, send_sem=send_sem.at[index], recv_sem=recv_sem.at[index],
            device_id=target, device_id_type=MESH,
        )
    return make


def refine_kernel(counts, rows_in, cols, obj_in, probe_in, meas_in, dft_in, object_out, probe_out,
                  obj, probe, meas, dft, block, ext, modes, powers,
                  from_cols, from_rows, to_rows, narrow, by, kept_light,
                  patch, factor, spec, light, terms, to_cols, total, grads,
                  out_probe, got_probe, out_power, got_power, pieces, got_y, whole_power, got_power_y,
                  wide, bands, got_z, rims, got_x, last_power, got_power_x,
                  out_light, got_light, far_light, far_got_light, halo_light, halo_got_light,
                  out_grad, got_grad, far_grad, far_got_grad, halo_grad, halo_got_grad,
                  send_sem, recv_sem, load_sem):
    loads = [
        pltpu.make_async_copy(src, dst, load_sem.at[i])
        for i, (src, dst) in enumerate(
            ((obj_in, obj), (probe_in, probe), (meas_in, meas), (dft_in, dft))
        )
    ]
    for load in loads:
        load.start()
    slots = 3
    tile, group, x, y, z, core = here()
    tiles = X * Y * Z // 2
    x_hi = group // 2
    sibling = device(x, y, z, 1 - core)
    opposite = device((x + 2) % X, y, z, core)
    before, after = (tile + tiles - 1) % tiles, (tile + 1) % tiles
    other = (group + 2) % 4
    halo_to = [
        {"tile": before, "mode": group}, {"tile": before, "mode": other},
        {"tile": after, "mode": group}, {"tile": after, "mode": other},
    ]
    along_x = [device((x + i) % X, y, z, core) for i in (1, 3, 2)]
    along_z = [device(x, y, (z + i) % Z, core) for i in range(1, Z)]
    make = sender(send_sem, recv_sem)

    across = device(X - 1 - x, y, z, core)
    along_y = [device(x, (y + i) % Y, z, core) for i in (1, 3, 2)]
    partners = [sibling] + halo_to + along_x + along_y + along_z
    barrier = pltpu.get_barrier_semaphore()
    for partner in partners:
        pl.semaphore_signal(barrier, inc=1, device_id=partner, device_id_type=MESH)
    rows = [jnp.where(group * slots + s < counts[0], rows_in[s], 4096) for s in range(slots)]

    mine = pl.multiple_of(group * 128, 128)
    theirs = pl.multiple_of(other * 128, 128)
    loads[0].wait()
    block[...] = obj[...].astype(bf)
    ext[:, pl.ds(mine, 128), 128:640] = block[...]

    @pl.when(tile == 0)
    def _():
        ext[:, :, :128] = jnp.zeros((2, 512, 128), bf)

    @pl.when(tile == tiles - 1)
    def _():
        ext[:, :, 640:] = jnp.zeros((2, 512, 128), bf)

    loads[1].wait()
    for k in range(2):
        for c in range(2):
            modes[group, 2 * k + c] = probe[k, c].astype(bf)
    pl.semaphore_wait(barrier, len(partners))

    def strip(start, low, width):
        return ext.at[:, pl.ds(start, 128), pl.ds(low, width)]

    def plane(which, index):
        return modes.at[which, pl.ds(index, 1)]

    cut = make(41, plane(group, y), plane(group, y), across)
    cut.start()
    own = make(47, modes.at[group], modes.at[group], sibling)
    own.start()
    far = make(40, block, strip(mine, 128, 512), opposite)
    far.start()
    left, right = block.at[:, :, pl.ds(0, 128)], block.at[:, :, pl.ds(384, 128)]
    halo = [
        make(42, left, strip(mine, 640, 128), halo_to[0]),
        make(43, left, strip(mine, 640, 128), halo_to[1]),
        make(44, right, strip(mine, 0, 128), halo_to[2]),
        make(45, right, strip(mine, 0, 128), halo_to[3]),
    ]
    sends = (tile > 0, tile > 0, tile < tiles - 1, tile < tiles - 1)
    gets = (tile < tiles - 1, tile < tiles - 1, tile > 0, tile > 0)
    for flag, copy in zip(sends, halo):
        pl.when(flag)(copy.start)
    near = make(46, block, strip(mine, 128, 512), sibling)
    near.start()

    def pass_on(index, ref):
        copy = make(index, ref, ref, sibling)
        copy.start()
        return copy

    def picks(height, width, shift, down):
        high = lax.broadcasted_iota(jnp.int32, (height, width), 0)
        wide = lax.broadcasted_iota(jnp.int32, (height, width), 1)
        hit = high == wide + shift if down else wide == high + shift
        return jnp.where(hit, 1.0, 0.0).astype(bf)

    def sorted_by_parity(down):
        high = lax.broadcasted_iota(jnp.int32, (N, N), 0)
        wide = lax.broadcasted_iota(jnp.int32, (N, N), 1)
        place, held = (high, wide) if down else (wide, high)
        hit = held == jnp.where(place < N // 2, 2 * place, 2 * place - (N - 1))
        return jnp.where(hit, 1.0, 0.0).astype(f32)

    for s in range(slots):
        from_cols[s] = picks(768, N, cols[s], True)
        from_rows[s] = picks(N, 512, rows[s], False)
        to_rows[s] = picks(512, N, rows[s], True)
        to_cols[s * N:(s + 1) * N, :] = picks(N, 768, cols[s], False)
    light[...] = jnp.zeros_like(light)
    wide[...] = jnp.zeros_like(wide)
    powers[...] = jnp.zeros_like(powers)
    grads[...] = jnp.zeros_like(grads)
    loads[2].wait()
    for s in range(slots):
        by_cols = jnp.dot(meas[s], sorted_by_parity(False), precision=lax.Precision.HIGHEST,
                          preferred_element_type=f32)
        meas[s] = jnp.dot(sorted_by_parity(True), by_cols, precision=lax.Precision.HIGHEST,
                          preferred_element_type=f32)

    def scatter(c):
        spread_rows = [dot(to_rows[s], terms[s]).astype(bf) for s in range(slots)]
        total[c] = dot(jnp.concatenate(spread_rows, 1), to_cols[...])

    def sibling_rows(c, out, k):
        for h in range(2):
            start = pl.multiple_of((2 * h + 1 - core) * 128, 128)
            out[h, k] = total[c, pl.ds(start, 128), :].astype(bf)

    def own_rows(c, h, got, k):
        start = pl.multiple_of((2 * h + core) * 128, 128)
        return total[c, pl.ds(start, 128), :] + got[h, k].astype(f32)

    def fan_out(first, far, far_got, halo, halo_got):
        copies = [
            make(first, far.at[:, :, pl.ds(128, 512)], far_got, opposite),
            make(first + 1, halo.at[0], halo_got.at[0], halo_to[0]),
            make(first + 2, far.at[:, :, pl.ds(0, 128)], halo_got.at[1], halo_to[1]),
            make(first + 3, halo.at[1], halo_got.at[2], halo_to[2]),
            make(first + 4, far.at[:, :, pl.ds(640, 128)], halo_got.at[3], halo_to[3]),
        ]
        for copy in copies:
            copy.start()
        return copies

    keep_left = jnp.where(tile > 0, 1.0, 0.0)
    keep_right = jnp.where(tile < tiles - 1, 1.0, 0.0)

    def merged(kept, far_got, halo_got, k):
        center = kept[:, 128:640] + far_got[k].astype(f32)
        from_right = (halo_got[0, k].astype(f32) + halo_got[1, k].astype(f32)) * keep_right
        from_left = (halo_got[2, k].astype(f32) + halo_got[3, k].astype(f32)) * keep_left
        return jnp.concatenate(
            [center[:, :128] + from_left, center[:, 128:384], center[:, 384:] + from_right], 1
        )

    cut.wait_recv()
    around = []
    for i, target in enumerate(along_y):
        copy = make(48 + i, plane(other, y), plane(other, y), target)
        copy.start()
        around.append(copy)
    planes_on = [pass_on(51, plane(other, y))]

    def narrow_rows(which):
        start = pl.multiple_of(which * 128, 128)
        for s in range(slots):
            for c in range(2):
                narrow[s, c, pl.ds(start, 128), :] = dot(
                    ext[c, pl.ds(start, 128), :], from_cols[s]
                ).astype(bf)

    halo_kept = []
    for i, (flag, start, low) in enumerate(
        zip(gets, (mine, theirs, mine, theirs), (640, 640, 0, 0))
    ):
        halo_kept.append((flag, make(52 + i, strip(start, low, 128), strip(start, low, 128), sibling)))

    def halo_on(i):
        flag, on = halo_kept[i]

        @pl.when(flag)
        def _():
            halo[i].wait_recv()
            on.start()

    def halo_in(i):
        flag, on = halo_kept[i]
        pl.when(flag)(on.wait_recv)

    halo_on(0)
    halo_on(2)
    narrow_rows(group)
    near.wait_recv()
    halo_in(0)
    halo_in(2)
    narrow_rows(group + 1 - 2 * core)
    halo_on(1)
    halo_on(3)
    far.wait_recv()
    far_on = pass_on(56, strip(theirs, 128, 512))
    narrow_rows(other)
    far_on.wait_recv()
    halo_in(1)
    halo_in(3)
    narrow_rows((other // 2) * 2 + 1 - core)
    for s in range(slots):
        for c in range(2):
            patch[s, c] = dot(from_rows[s], narrow[s, c])
    factor[0] = patch[0, 0] * patch[0, 0] + patch[0, 1] * patch[0, 1]
    for s in range(1, slots):
        factor[0] += patch[s, 0] * patch[s, 0] + patch[s, 1] * patch[s, 1]
    out_power[...] = factor[0].astype(bf)
    power_copy = make(0, out_power, got_power, sibling)
    power_copy.start()
    loads[3].wait()

    def spectra(q, g):
        m = 2 * g + q
        pr = modes[m // 2, 2 * (m % 2)].astype(f32)
        pi = modes[m // 2, 2 * (m % 2) + 1].astype(f32)
        added, taken = [], []
        for s in range(slots):
            re = pr * patch[s, 0] - pi * patch[s, 1]
            im = pr * patch[s, 1] + pi * patch[s, 0]
            added.append(side([re[:, :H] + re[:, H:], im[:, :H] + im[:, H:]]).astype(bf))
            taken.append(side([re[:, :H] - re[:, H:], im[:, :H] - im[:, H:]]).astype(bf))
        even = dot(stack(added), dft[0])
        odd = dot(stack(taken), dft[1])
        added, taken = [], []
        for s in range(slots):
            low, high = slice(s * N, s * N + H), slice(s * N + H, (s + 1) * N)
            e, o = even[low] + even[high], odd[low] + odd[high]
            added.append(stack([side([e[:, :H], o[:, :H]]), side([e[:, H:], o[:, H:]])]).astype(bf))
            e, o = even[low] - even[high], odd[low] - odd[high]
            taken.append(stack([side([e[:, :H], o[:, :H]]), side([e[:, H:], o[:, H:]])]).astype(bf))
        even = dot(dft[2], side(added))
        odd = dot(dft[3], side(taken))
        spec[m, :N] = even
        spec[m, N:] = odd
        for s in range(slots):
            e, o = even[:, s * N:(s + 1) * N], odd[:, s * N:(s + 1) * N]
            powers[s, :H] += e[:H] * e[:H] + e[H:] * e[H:]
            powers[s, H:] += o[:H] * o[:H] + o[H:] * o[H:]
        return g

    def mode_light(g):
        for k in range(2):
            re = modes[g, 2 * k].astype(f32)
            im = modes[g, 2 * k + 1].astype(f32)
            light[...] += re * re + im * im

    near_group = group + 1 - 2 * core
    lax.fori_loop(0, 2, spectra, group, unroll=True)
    for i, step in enumerate((1, 3, 2)):
        around[i].wait_recv()
        planes_on.append(pass_on(57 + i, plane(other, (y + Y - step) % Y)))
    own.wait_recv()
    lax.fori_loop(0, 2, spectra, near_group, unroll=True)
    mode_light(group)
    mode_light(near_group)
    for copy in planes_on:
        copy.wait_recv()
    lax.fori_loop(0, 2, spectra, other, unroll=True)
    lax.fori_loop(0, 2, spectra, (near_group + 2) % 4, unroll=True)
    mode_light(other)
    mode_light((near_group + 2) % 4)
    for s in range(slots):
        terms[s] = light[...].astype(bf)
    scatter(0)
    sibling_rows(0, out_light, 0)
    light_copy = make(1, out_light, got_light, sibling)
    light_copy.start()
    for s in range(slots):
        ratio = meas[s] * lax.rsqrt(jnp.maximum(powers[s], 0.25)) - 1.0
        for p in range(2):
            rows_p = ratio[p * H:(p + 1) * H]
            by[p, :, s * N:(s + 1) * N] = stack([rows_p, rows_p])


    def passed(i):
        return make(60 + i, out_probe.at[i], got_probe.at[i], sibling)

    def to_y(i, j):
        k = 3 * i + j - 1
        return make(70 + k, pieces.at[i, :, :, (y + j) % Y], got_y.at[k], device(x, (y + j) % Y, z, core))

    def power_y(j):
        return make(82 + j, whole_power.at[:, (y + j) % Y], got_power_y.at[j - 1],
                    device(x, (y + j) % Y, z, core))

    def to_z(h, i):
        height = 48 if h == 0 else 32
        return make(
            86 + 8 * h + i, bands.at[h, (z + i) % Z, pl.ds(0, height)],
            got_z.at[h, i, pl.ds(0, height)], along_z[i - 1]
        )

    def to_x(h, xl):
        i = (2 * h + xl - x + X) % X
        return make(104 + i, rims.at[h, pl.ds(16 * xl, 16)], got_x.at[i], device(2 * h + xl, y, z, core)), i

    def power_x(i):
        return make(108 + i, last_power.at[(x + i) % 2], got_power_x.at[i], device((x + i) % X, y, z, core))

    def reduce_y(h):
        for p in range(2):
            i = 2 * h + p
            band = pieces[i, :, :, y].astype(f32)
            for j in range(1, Y):
                to_y(i, j).wait_recv()
                band = band + got_y[3 * i + j - 1].astype(f32)
            for part in range(Z):
                for xl in range(2):
                    for c in range(2):
                        at = 16 * xl + 8 * p + 4 * c
                        wide[part, at:at + 4] = band[c, xl, 4 * part:4 * part + 4]
        if h == 0:
            band = whole_power[:, y].astype(f32)
            for j in range(1, Y):
                power_y(j).wait_recv()
                band = band + got_power_y[j - 1].astype(f32)
            for part in range(Z):
                for xl in range(2):
                    wide[part, 32 + 4 * xl:36 + 4 * xl] = band[xl, 4 * part:4 * part + 4]
        bands[h] = wide[...].astype(bf)
        for i in range(1, Z):
            to_z(h, i).start()

    def reduce_z(h):
        height = 48 if h == 0 else 32
        total_z = bands[h, z, :height].astype(f32)
        for i in range(1, Z):
            to_z(h, i).wait_recv()
            total_z = total_z + got_z[h, i, :height].astype(f32)
        rims[h] = total_z[:32]
        for xl in range(2):
            copy, i = to_x(h, xl)
            pl.when(i > 0)(copy.start)
        if h == 0:
            for xl in range(2):
                last_power[xl, :4] = total_z[32 + 4 * xl:36 + 4 * xl]
                last_power[xl, 4:] = total_z[36:40]
            for i in range(1, X):
                power_x(i).start()

    def back_step(step, _):
        i = step // 2
        m = 4 * (i // 2) + 2 * jnp.where(step % 2 == 0, 1 - core, core) + i % 2
        pr = modes[m // 2, 2 * (m % 2)].astype(f32)
        pi = modes[m // 2, 2 * (m % 2) + 1].astype(f32)
        even = dot(dft[4], (spec[m, :N] * by[0]).astype(bf))
        odd = dot(dft[5], (spec[m, N:] * by[1]).astype(bf))
        low, high = (even + odd).astype(bf), (even - odd).astype(bf)
        at_even, at_odd = [], []
        for s in range(slots):
            c, d = slice(s * N, s * N + H), slice(s * N + H, (s + 1) * N)
            at_even.append(side([stack([low[:H, c], high[:H, c]]), stack([low[H:, c], high[H:, c]])]))
            at_odd.append(side([stack([low[:H, d], high[:H, d]]), stack([low[H:, d], high[H:, d]])]))
        even = dot(stack(at_even), dft[6])
        odd = dot(stack(at_odd), dft[7])
        low, high = even + odd, even - odd
        sum_re, sum_im = None, None
        for s in range(slots):
            r = slice(s * N, (s + 1) * N)
            br = side([low[r, :H], high[r, :H]])
            bi = side([low[r, H:], high[r, H:]])
            ar = patch[s, 0]
            ai = patch[s, 1]
            re = ar * br + ai * bi
            im = ar * bi - ai * br
            sum_re = re if s == 0 else sum_re + re
            sum_im = im if s == 0 else sum_im + im
            grads[s, 0] += pr * br + pi * bi
            grads[s, 1] += pr * bi - pi * br

        @pl.when(step % 2 == 0)
        def _():
            out_probe[i, 0] = sum_re.astype(bf)
            out_probe[i, 1] = sum_im.astype(bf)
            passed(i).start()

        @pl.when(step % 2 == 1)
        def _():
            passed(i).wait_recv()
            for c, mine_sum in enumerate((sum_re, sum_im)):
                both = (mine_sum + got_probe[i, c].astype(f32)).astype(bf)
                pieces[i, c] = both.reshape(2, Y, 32, N)
            for j in range(1, Y):
                to_y(i, j).start()
        return 0

    power_copy.wait_recv()
    whole_power[...] = (out_power[...].astype(f32) + got_power[...].astype(f32)).astype(bf).reshape(2, Y, 32, N)
    for j in range(1, Y):
        power_y(j).start()
    lax.fori_loop(0, 2, back_step, 0)
    light_copy.wait_recv()
    kept = own_rows(0, x_hi, got_light, 0)
    kept_light[...] = kept
    far_light[0] = own_rows(0, 1 - x_hi, got_light, 0).astype(bf)
    halo_light[0, 0] = kept[:, :128].astype(bf)
    halo_light[1, 0] = kept[:, 640:].astype(bf)
    light_copies = fan_out(2, far_light, far_got_light, halo_light, halo_got_light)
    lax.fori_loop(2, 8, back_step, 0)

    for copy in light_copies:
        copy.wait_recv()
    weight = merged(kept_light[...], far_got_light, halo_got_light, 0) + object_reg

    for c in range(2):
        for s in range(slots):
            terms[s] = grads[s, c].astype(bf)
        scatter(c)
    for c in range(2):
        sibling_rows(c, out_grad, c)
    grad_copy = make(32, out_grad, got_grad, sibling)
    grad_copy.start()
    reduce_y(0)
    grad_copy.wait_recv()
    for c in range(2):
        far_grad[c] = own_rows(c, 1 - x_hi, got_grad, c).astype(bf)
        halo_grad[0, c] = own_rows(c, x_hi, got_grad, c)[:, :128].astype(bf)
        halo_grad[1, c] = own_rows(c, x_hi, got_grad, c)[:, 640:].astype(bf)
    grad_copies = fan_out(33, far_grad, far_got_grad, halo_grad, halo_got_grad)

    reduce_y(1)
    reduce_z(0)
    reduce_z(1)
    for copy in grad_copies:
        copy.wait_recv()
    for c in range(2):
        kept = own_rows(c, x_hi, got_grad, c)
        object_out[c] = obj[c] + merged(kept, far_got_grad, halo_got_grad, c) / weight

    final = rims[x_hi, pl.ds(pl.multiple_of(16 * (x % 2), 16), 16)]
    weight = last_power[x % 2, :4] + probe_reg
    for i in range(1, X):
        make(104 + i, rims.at[0, pl.ds(0, 16)], got_x.at[i], sibling).wait_recv()
        final = final + got_x[i]
        power_x(i).wait_recv()
        weight = weight + got_power_x[i, :4]
    at = pl.multiple_of((tile // 2) * 8, 8)
    for k in range(4):
        rows8 = probe[k // 2, k % 2, pl.ds(at, 8), :]
        probe_row = jnp.where(tile % 2 == 0, rows8[:4], rows8[4:])
        probe_out[k] = probe_row + final[4 * k:4 * k + 4] / weight
    for copy in [far, cut, near, own, far_on] + around + planes_on:
        copy.wait_send()
    for flag, copy in zip(sends, halo):
        pl.when(flag)(copy.wait_send)
    for flag, copy in halo_kept:
        pl.when(flag)(copy.wait_send)
    for copy in [power_copy, light_copy, grad_copy, ] + light_copies + grad_copies:
        copy.wait_send()
    for i in range(4):
        passed(i).wait_send()
        for j in range(1, Y):
            to_y(i, j).wait_send()
    for h in range(2):
        for i in range(1, Z):
            to_z(h, i).wait_send()
    for j in range(1, Y):
        power_y(j).wait_send()
    for i in range(1, X):
        make(104 + i, rims.at[0, pl.ds(0, 16)], got_x.at[i], sibling).wait_send()
        power_x(i).wait_send()


def refine(counts, rows, cols, obj, probe, meas):
    whole = pl.BlockSpec(memory_space=pltpu.VMEM)
    scalars = pl.BlockSpec(memory_space=pltpu.SMEM)
    remote = pl.BlockSpec(memory_space=pl.ANY)
    return pl.pallas_call(
        refine_kernel,
        out_shape=(
            jax.ShapeDtypeStruct((2, 128, 512), f32), jax.ShapeDtypeStruct((4, 4, N), f32)
        ),
        in_specs=[scalars] * 3 + [remote] * 4,
        out_specs=(whole, whole),
        scratch_shapes=[
            pltpu.VMEM((2, 128, 512), f32),
            pltpu.VMEM((2, 2, N, N), f32),
            pltpu.VMEM((3, N, N), f32),
            pltpu.VMEM((8, N, N), bf),
            pltpu.VMEM((2, 128, 512), bf),
            pltpu.VMEM((2, 512, 768), bf),
            pltpu.VMEM((4, 4, N, N), bf),
            pltpu.VMEM((3, N, N), f32),
            pltpu.VMEM((3, 768, N), bf),
            pltpu.VMEM((3, N, 512), bf),
            pltpu.VMEM((3, 512, N), bf),
            pltpu.VMEM((3, 2, 512, N), bf),
            pltpu.VMEM((2, N, 3 * N), f32),
            pltpu.VMEM((128, 768), f32),
            pltpu.VMEM((3, 2, N, N), f32),
            pltpu.VMEM((3, N, N), f32),
            pltpu.VMEM((8, 2 * N, 3 * N), f32),
            pltpu.VMEM((N, N), f32),
            pltpu.VMEM((3, N, N), bf),
            pltpu.VMEM((3 * N, 768), bf),
            pltpu.VMEM((2, 512, 768), f32),
            pltpu.VMEM((3, 2, N, N), f32),
            pltpu.VMEM((4, 2, N, N), bf),
            pltpu.VMEM((4, 2, N, N), bf),
            pltpu.VMEM((N, N), bf),
            pltpu.VMEM((N, N), bf),
            pltpu.VMEM((4, 2, 2, Y, 32, N), bf),
            pltpu.VMEM((12, 2, 2, 32, N), bf),
            pltpu.VMEM((2, Y, 32, N), bf),
            pltpu.VMEM((3, 2, 32, N), bf),
            pltpu.VMEM((Z, 48, N), f32),
            pltpu.VMEM((2, Z, 48, N), bf),
            pltpu.VMEM((2, Z, 48, N), bf),
            pltpu.VMEM((2, 32, N), f32),
            pltpu.VMEM((X, 16, N), f32),
            pltpu.VMEM((2, 8, N), f32),
            pltpu.VMEM((X, 8, N), f32),
            pltpu.VMEM((2, 1, 128, 768), bf),
            pltpu.VMEM((2, 1, 128, 768), bf),
            pltpu.VMEM((1, 128, 768), bf),
            pltpu.VMEM((1, 128, 512), bf),
            pltpu.VMEM((2, 1, 128, 128), bf),
            pltpu.VMEM((4, 1, 128, 128), bf),
            pltpu.VMEM((2, 2, 128, 768), bf),
            pltpu.VMEM((2, 2, 128, 768), bf),
            pltpu.VMEM((2, 128, 768), bf),
            pltpu.VMEM((2, 128, 512), bf),
            pltpu.VMEM((2, 2, 128, 128), bf),
            pltpu.VMEM((4, 2, 128, 128), bf),
            pltpu.SemaphoreType.DMA((112,)), pltpu.SemaphoreType.DMA((112,)),
            pltpu.SemaphoreType.DMA((4,)),
        ],
        compiler_params=pltpu.CompilerParams(
            collective_id=1, has_side_effects=True, vmem_limit_bytes=60 * 2**20
        ),
        name="refine",
    )(counts, rows, cols, obj, probe, meas, jnp.asarray(tables()))


def local(object_field, probe, measured, scan_rows, scan_cols, counts):
    object_out, probe_out = refine(counts, scan_rows, scan_cols, object_field, probe, measured)
    return object_out, probe_out.reshape(2, 2, 4, N)


def solution(mesh):
    return jax.shard_map(
        local,
        mesh=mesh,
        in_specs=(
            P(None, "mode", "tile"),
            P("mode", None, None, None),
            P(("tile", "mode"), None, None),
            P(("tile", "mode")),
            P(("tile", "mode")),
            P("tile"),
        ),
        out_specs=(P(None, "mode", "tile"), P("mode", None, "tile", None)),
        check_vma=False,
    )
```

```python
import functools

import jax
import jax.numpy as jnp
import ml_dtypes
import numpy as np
from jax import lax
from jax.experimental import pallas as pl
from jax.experimental.pallas import tpu as pltpu
from jax.sharding import PartitionSpec as P

object_reg = 0.5
probe_reg = 1.0
N = 256
H = N // 2
X, Y, Z = 4, 4, 8
bf = jnp.bfloat16
f32 = jnp.float32
MESH = pl.DeviceIdType.MESH


def tables():
    pos = np.arange(N)
    ang = (pos[:, None] * pos[None, :] % N) * (2.0 * np.pi / N)
    sc = 1.0 / np.sqrt(float(N))
    re = (np.cos(ang) * sc).astype(ml_dtypes.bfloat16)
    im = (-np.sin(ang) * sc).astype(ml_dtypes.bfloat16)
    out = []
    for p in range(2):
        c, s = re[:H, p::2], im[:H, p::2]
        out.append(np.block([[c, s], [-s, c]]))
    for p in range(2):
        c, s = re[p::2, :H], im[p::2, :H]
        out.append(np.block([[c, -s], [s, c]]))
    for p in range(2):
        c, s = re[:H, p::2], im[:H, p::2]
        out.append(np.block([[c, s], [-s, c]]))
    for p in range(2):
        c, s = re[p::2, :H], im[p::2, :H]
        out.append(np.block([[c, -s], [s, c]]))
    return np.stack(out).astype(ml_dtypes.bfloat16)


def side(parts):
    return jnp.concatenate(parts, 1)


def stack(parts):
    return jnp.concatenate(parts, 0)


def dot(a, b):
    return jnp.dot(a, b, preferred_element_type=f32)


def here():
    tile = lax.axis_index("tile")
    group = lax.axis_index("mode")
    x = (group // 2) * 2 + tile // (Y * Z)
    return tile, group, x, (tile // Z) % Y, tile % Z, group % 2


def device(x, y, z, core):
    return {"tile": (x % 2) * (Y * Z) + y * Z + z, "mode": (x // 2) * 2 + core}


def sender(send_sem, recv_sem):
    def make(index, src, dst, target):
        return pltpu.make_async_remote_copy(
            src_ref=src, dst_ref=dst, send_sem=send_sem.at[index], recv_sem=recv_sem.at[index],
            device_id=target, device_id_type=MESH,
        )
    return make


def refine_kernel(counts, rows_in, cols, obj_in, probe_in, meas_in, dft_in, object_out, probe_out,
                  obj, probe, meas, dft, block, ext, modes, powers,
                  from_cols, from_rows, to_rows, narrow, by, kept_light,
                  patch, factor, spec, light, terms, to_cols, total, grads,
                  out_probe, got_probe, out_power, got_power, pieces, got_y, whole_power, got_power_y,
                  wide, bands, got_z, rims, got_x, last_power, got_power_x,
                  out_light, got_light, far_light, far_got_light, halo_light, halo_got_light,
                  out_grad, got_grad, far_grad, far_got_grad, halo_grad, halo_got_grad,
                  send_sem, recv_sem, load_sem):
    loads = [
        pltpu.make_async_copy(src, dst, load_sem.at[i])
        for i, (src, dst) in enumerate(
            ((obj_in, obj), (probe_in, probe), (meas_in, meas), (dft_in, dft))
        )
    ]
    for load in loads:
        load.start()
    slots = 3
    tile, group, x, y, z, core = here()
    tiles = X * Y * Z // 2
    x_hi = group // 2
    sibling = device(x, y, z, 1 - core)
    opposite = device((x + 2) % X, y, z, core)
    before, after = (tile + tiles - 1) % tiles, (tile + 1) % tiles
    other = (group + 2) % 4
    halo_to = [
        {"tile": before, "mode": group}, {"tile": before, "mode": other},
        {"tile": after, "mode": group}, {"tile": after, "mode": other},
    ]
    along_x = [device((x + i) % X, y, z, core) for i in (1, 3, 2)]
    along_z = [device(x, y, (z + i) % Z, core) for i in range(1, Z)]
    make = sender(send_sem, recv_sem)

    across = device(X - 1 - x, y, z, core)
    along_y = [device(x, (y + i) % Y, z, core) for i in (2, 1, 3)]
    partners = [sibling] + halo_to + along_x + along_y + along_z
    barrier = pltpu.get_barrier_semaphore()
    for partner in partners:
        pl.semaphore_signal(barrier, inc=1, device_id=partner, device_id_type=MESH)
    rows = [jnp.where(group * slots + s < counts[0], rows_in[s], 4096) for s in range(slots)]

    mine = pl.multiple_of(group * 128, 128)
    theirs = pl.multiple_of(other * 128, 128)
    loads[0].wait()
    block[...] = obj[...].astype(bf)
    ext[:, pl.ds(mine, 128), 128:640] = block[...]

    @pl.when(tile == 0)
    def _():
        ext[:, :, :128] = jnp.zeros((2, 512, 128), bf)

    @pl.when(tile == tiles - 1)
    def _():
        ext[:, :, 640:] = jnp.zeros((2, 512, 128), bf)

    loads[1].wait()
    for k in range(2):
        for c in range(2):
            modes[group, 2 * k + c] = probe[k, c].astype(bf)
    pl.semaphore_wait(barrier, len(partners))

    def strip(start, low, width):
        return ext.at[:, pl.ds(start, 128), pl.ds(low, width)]

    def plane(which, index):
        return modes.at[which, pl.ds(index, 1)]

    cut = make(41, plane(group, y), plane(group, y), across)
    cut.start()
    own = make(47, modes.at[group], modes.at[group], sibling)
    own.start()
    far = make(40, block, strip(mine, 128, 512), opposite)
    far.start()
    left, right = block.at[:, :, pl.ds(0, 128)], block.at[:, :, pl.ds(384, 128)]
    halo = [
        make(42, left, strip(mine, 640, 128), halo_to[0]),
        make(43, left, strip(mine, 640, 128), halo_to[1]),
        make(44, right, strip(mine, 0, 128), halo_to[2]),
        make(45, right, strip(mine, 0, 128), halo_to[3]),
    ]
    sends = (tile > 0, tile > 0, tile < tiles - 1, tile < tiles - 1)
    gets = (tile < tiles - 1, tile < tiles - 1, tile > 0, tile > 0)
    for i in (1, 3, 0, 2):
        pl.when(sends[i])(halo[i].start)
    near = make(46, block, strip(mine, 128, 512), sibling)
    near.start()

    def pass_on(index, ref):
        copy = make(index, ref, ref, sibling)
        copy.start()
        return copy

    def picks(height, width, shift, down):
        high = lax.broadcasted_iota(jnp.int32, (height, width), 0)
        wide = lax.broadcasted_iota(jnp.int32, (height, width), 1)
        hit = high == wide + shift if down else wide == high + shift
        return jnp.where(hit, 1.0, 0.0).astype(bf)

    def sorted_by_parity(down):
        high = lax.broadcasted_iota(jnp.int32, (N, N), 0)
        wide = lax.broadcasted_iota(jnp.int32, (N, N), 1)
        place, held = (high, wide) if down else (wide, high)
        hit = held == jnp.where(place < N // 2, 2 * place, 2 * place - (N - 1))
        return jnp.where(hit, 1.0, 0.0).astype(f32)

    for s in range(slots):
        from_cols[s] = picks(768, N, cols[s], True)
        from_rows[s] = picks(N, 512, rows[s], False)
        to_rows[s] = picks(512, N, rows[s], True)
        to_cols[s * N:(s + 1) * N, :] = picks(N, 768, cols[s], False)
    light[...] = jnp.zeros_like(light)
    wide[...] = jnp.zeros_like(wide)
    powers[...] = jnp.zeros_like(powers)
    grads[...] = jnp.zeros_like(grads)
    loads[2].wait()
    for s in range(slots):
        by_cols = jnp.dot(meas[s], sorted_by_parity(False), precision=lax.Precision.HIGHEST,
                          preferred_element_type=f32)
        meas[s] = jnp.dot(sorted_by_parity(True), by_cols, precision=lax.Precision.HIGHEST,
                          preferred_element_type=f32)

    def scatter(c):
        spread_rows = [dot(to_rows[s], terms[s]).astype(bf) for s in range(slots)]
        total[c] = dot(jnp.concatenate(spread_rows, 1), to_cols[...])

    def sibling_rows(c, out, k):
        for h in range(2):
            start = pl.multiple_of((2 * h + 1 - core) * 128, 128)
            out[h, k] = total[c, pl.ds(start, 128), :].astype(bf)

    def own_rows(c, h, got, k):
        start = pl.multiple_of((2 * h + core) * 128, 128)
        return total[c, pl.ds(start, 128), :] + got[h, k].astype(f32)

    def fan_out(first, far, far_got, halo, halo_got):
        copies = [
            make(first, far.at[:, :, pl.ds(128, 512)], far_got, opposite),
            make(first + 1, halo.at[0], halo_got.at[0], halo_to[0]),
            make(first + 2, far.at[:, :, pl.ds(0, 128)], halo_got.at[1], halo_to[1]),
            make(first + 3, halo.at[1], halo_got.at[2], halo_to[2]),
            make(first + 4, far.at[:, :, pl.ds(640, 128)], halo_got.at[3], halo_to[3]),
        ]
        for copy in copies:
            copy.start()
        return copies

    keep_left = jnp.where(tile > 0, 1.0, 0.0)
    keep_right = jnp.where(tile < tiles - 1, 1.0, 0.0)

    def merged(kept, far_got, halo_got, k):
        center = kept[:, 128:640] + far_got[k].astype(f32)
        from_right = (halo_got[0, k].astype(f32) + halo_got[1, k].astype(f32)) * keep_right
        from_left = (halo_got[2, k].astype(f32) + halo_got[3, k].astype(f32)) * keep_left
        return jnp.concatenate(
            [center[:, :128] + from_left, center[:, 128:384], center[:, 384:] + from_right], 1
        )

    cut.wait_recv()
    around = []
    for i, target in enumerate(along_y):
        copy = make(48 + i, plane(other, y), plane(other, y), target)
        copy.start()
        around.append(copy)
    planes_on = [pass_on(51, plane(other, y))]

    def narrow_rows(which):
        start = pl.multiple_of(which * 128, 128)
        for s in range(slots):
            for c in range(2):
                narrow[s, c, pl.ds(start, 128), :] = dot(
                    ext[c, pl.ds(start, 128), :], from_cols[s]
                ).astype(bf)

    halo_kept = []
    for i, (flag, start, low) in enumerate(
        zip(gets, (mine, theirs, mine, theirs), (640, 640, 0, 0))
    ):
        halo_kept.append((flag, make(52 + i, strip(start, low, 128), strip(start, low, 128), sibling)))

    def halo_on(i):
        flag, on = halo_kept[i]

        @pl.when(flag)
        def _():
            halo[i].wait_recv()
            on.start()

    def halo_in(i):
        flag, on = halo_kept[i]
        pl.when(flag)(on.wait_recv)

    halo_on(0)
    halo_on(2)
    narrow_rows(group)
    near.wait_recv()
    halo_in(0)
    halo_in(2)
    narrow_rows(group + 1 - 2 * core)
    halo_on(1)
    halo_on(3)
    far.wait_recv()
    far_on = pass_on(56, strip(theirs, 128, 512))
    narrow_rows(other)
    far_on.wait_recv()
    halo_in(1)
    halo_in(3)
    narrow_rows((other // 2) * 2 + 1 - core)
    for s in range(slots):
        for c in range(2):
            patch[s, c] = dot(from_rows[s], narrow[s, c])
    factor[0] = patch[0, 0] * patch[0, 0] + patch[0, 1] * patch[0, 1]
    for s in range(1, slots):
        factor[0] += patch[s, 0] * patch[s, 0] + patch[s, 1] * patch[s, 1]
    out_power[...] = factor[0].astype(bf)
    power_copy = make(0, out_power, got_power, sibling)
    power_copy.start()
    loads[3].wait()

    def spectra(q, g):
        m = 2 * g + q
        pr = modes[m // 2, 2 * (m % 2)].astype(f32)
        pi = modes[m // 2, 2 * (m % 2) + 1].astype(f32)
        added, taken = [], []
        for s in range(slots):
            re = pr * patch[s, 0] - pi * patch[s, 1]
            im = pr * patch[s, 1] + pi * patch[s, 0]
            added.append(side([re[:, :H] + re[:, H:], im[:, :H] + im[:, H:]]).astype(bf))
            taken.append(side([re[:, :H] - re[:, H:], im[:, :H] - im[:, H:]]).astype(bf))
        even = dot(stack(added), dft[0])
        odd = dot(stack(taken), dft[1])
        added, taken = [], []
        for s in range(slots):
            low, high = slice(s * N, s * N + H), slice(s * N + H, (s + 1) * N)
            e, o = even[low] + even[high], odd[low] + odd[high]
            added.append(stack([side([e[:, :H], o[:, :H]]), side([e[:, H:], o[:, H:]])]).astype(bf))
            e, o = even[low] - even[high], odd[low] - odd[high]
            taken.append(stack([side([e[:, :H], o[:, :H]]), side([e[:, H:], o[:, H:]])]).astype(bf))
        even = dot(dft[2], side(added))
        odd = dot(dft[3], side(taken))
        spec[m, :N] = even
        spec[m, N:] = odd
        for s in range(slots):
            e, o = even[:, s * N:(s + 1) * N], odd[:, s * N:(s + 1) * N]
            powers[s, :H] += e[:H] * e[:H] + e[H:] * e[H:]
            powers[s, H:] += o[:H] * o[:H] + o[H:] * o[H:]
        return g

    def mode_light(g):
        for k in range(2):
            re = modes[g, 2 * k].astype(f32)
            im = modes[g, 2 * k + 1].astype(f32)
            light[...] += re * re + im * im

    near_group = group + 1 - 2 * core
    lax.fori_loop(0, 2, spectra, group, unroll=True)
    for i, step in enumerate((2, 1, 3)):
        around[i].wait_recv()
        planes_on.append(pass_on(57 + i, plane(other, (y + Y - step) % Y)))
    own.wait_recv()
    lax.fori_loop(0, 2, spectra, near_group, unroll=True)
    mode_light(group)
    mode_light(near_group)
    for copy in planes_on:
        copy.wait_recv()
    lax.fori_loop(0, 2, spectra, other, unroll=True)
    lax.fori_loop(0, 2, spectra, (near_group + 2) % 4, unroll=True)
    mode_light(other)
    mode_light((near_group + 2) % 4)
    for s in range(slots):
        terms[s] = light[...].astype(bf)
    scatter(0)
    sibling_rows(0, out_light, 0)
    light_copy = make(1, out_light, got_light, sibling)
    light_copy.start()
    for s in range(slots):
        ratio = meas[s] * lax.rsqrt(jnp.maximum(powers[s], 0.25)) - 1.0
        for p in range(2):
            rows_p = ratio[p * H:(p + 1) * H]
            by[p, :, s * N:(s + 1) * N] = stack([rows_p, rows_p])


    def passed(i):
        return make(60 + i, out_probe.at[i], got_probe.at[i], sibling)

    def to_y(i, j):
        k = 3 * i + j - 1
        return make(70 + k, pieces.at[i, :, :, (y + j) % Y], got_y.at[k], device(x, (y + j) % Y, z, core))

    def power_y(j):
        return make(82 + j, whole_power.at[:, (y + j) % Y], got_power_y.at[j - 1],
                    device(x, (y + j) % Y, z, core))

    def to_z(h, i):
        height = 48 if h == 0 else 32
        return make(
            86 + 8 * h + i, bands.at[h, (z + i) % Z, pl.ds(0, height)],
            got_z.at[h, i, pl.ds(0, height)], along_z[i - 1]
        )

    def to_x(h, xl):
        i = (2 * h + xl - x + X) % X
        return make(104 + i, rims.at[h, pl.ds(16 * xl, 16)], got_x.at[i], device(2 * h + xl, y, z, core)), i

    def power_x(i):
        return make(108 + i, last_power.at[(x + i) % 2], got_power_x.at[i], device((x + i) % X, y, z, core))

    def reduce_y(h):
        for p in range(2):
            i = 2 * h + p
            band = pieces[i, :, :, y].astype(f32)
            for j in range(1, Y):
                to_y(i, j).wait_recv()
                band = band + got_y[3 * i + j - 1].astype(f32)
            for part in range(Z):
                for xl in range(2):
                    for c in range(2):
                        at = 16 * xl + 8 * p + 4 * c
                        wide[part, at:at + 4] = band[c, xl, 4 * part:4 * part + 4]
        if h == 0:
            band = whole_power[:, y].astype(f32)
            for j in range(1, Y):
                power_y(j).wait_recv()
                band = band + got_power_y[j - 1].astype(f32)
            for part in range(Z):
                for xl in range(2):
                    wide[part, 32 + 4 * xl:36 + 4 * xl] = band[xl, 4 * part:4 * part + 4]
        bands[h] = wide[...].astype(bf)
        for i in (4, 3, 5, 2, 6, 1, 7):
            to_z(h, i).start()

    def reduce_z(h):
        height = 48 if h == 0 else 32
        total_z = bands[h, z, :height].astype(f32)
        for i in range(1, Z):
            to_z(h, i).wait_recv()
            total_z = total_z + got_z[h, i, :height].astype(f32)
        rims[h] = total_z[:32]
        for xl in range(2):
            copy, i = to_x(h, xl)
            pl.when(i > 0)(copy.start)
        if h == 0:
            for xl in range(2):
                last_power[xl, :4] = total_z[32 + 4 * xl:36 + 4 * xl]
                last_power[xl, 4:] = total_z[36:40]
            for i in range(1, X):
                power_x(i).start()

    def back_step(step, _):
        i = step // 2
        m = 4 * (i // 2) + 2 * jnp.where(step % 2 == 0, 1 - core, core) + i % 2
        pr = modes[m // 2, 2 * (m % 2)].astype(f32)
        pi = modes[m // 2, 2 * (m % 2) + 1].astype(f32)
        even = dot(dft[4], (spec[m, :N] * by[0]).astype(bf))
        odd = dot(dft[5], (spec[m, N:] * by[1]).astype(bf))
        low, high = (even + odd).astype(bf), (even - odd).astype(bf)
        at_even, at_odd = [], []
        for s in range(slots):
            c, d = slice(s * N, s * N + H), slice(s * N + H, (s + 1) * N)
            at_even.append(side([stack([low[:H, c], high[:H, c]]), stack([low[H:, c], high[H:, c]])]))
            at_odd.append(side([stack([low[:H, d], high[:H, d]]), stack([low[H:, d], high[H:, d]])]))
        even = dot(stack(at_even), dft[6])
        odd = dot(stack(at_odd), dft[7])
        low, high = even + odd, even - odd
        sum_re, sum_im = None, None
        for s in range(slots):
            r = slice(s * N, (s + 1) * N)
            br = side([low[r, :H], high[r, :H]])
            bi = side([low[r, H:], high[r, H:]])
            ar = patch[s, 0]
            ai = patch[s, 1]
            re = ar * br + ai * bi
            im = ar * bi - ai * br
            sum_re = re if s == 0 else sum_re + re
            sum_im = im if s == 0 else sum_im + im
            grads[s, 0] += pr * br + pi * bi
            grads[s, 1] += pr * bi - pi * br

        @pl.when(step % 2 == 0)
        def _():
            out_probe[i, 0] = sum_re.astype(bf)
            out_probe[i, 1] = sum_im.astype(bf)
            passed(i).start()

        @pl.when(step % 2 == 1)
        def _():
            passed(i).wait_recv()
            for c, mine_sum in enumerate((sum_re, sum_im)):
                both = (mine_sum + got_probe[i, c].astype(f32)).astype(bf)
                pieces[i, c] = both.reshape(2, Y, 32, N)
            for j in (2, 1, 3):
                to_y(i, j).start()
        return 0

    power_copy.wait_recv()
    whole_power[...] = (out_power[...].astype(f32) + got_power[...].astype(f32)).astype(bf).reshape(2, Y, 32, N)
    for j in range(1, Y):
        power_y(j).start()
    lax.fori_loop(0, 2, back_step, 0)
    light_copy.wait_recv()
    kept = own_rows(0, x_hi, got_light, 0)
    kept_light[...] = kept
    far_light[0] = own_rows(0, 1 - x_hi, got_light, 0).astype(bf)
    halo_light[0, 0] = kept[:, :128].astype(bf)
    halo_light[1, 0] = kept[:, 640:].astype(bf)
    light_copies = fan_out(2, far_light, far_got_light, halo_light, halo_got_light)
    lax.fori_loop(2, 8, back_step, 0)

    for copy in light_copies:
        copy.wait_recv()
    weight = merged(kept_light[...], far_got_light, halo_got_light, 0) + object_reg

    for c in range(2):
        for s in range(slots):
            terms[s] = grads[s, c].astype(bf)
        scatter(c)
    for c in range(2):
        sibling_rows(c, out_grad, c)
    grad_copy = make(32, out_grad, got_grad, sibling)
    grad_copy.start()
    reduce_y(0)
    grad_copy.wait_recv()
    for c in range(2):
        far_grad[c] = own_rows(c, 1 - x_hi, got_grad, c).astype(bf)
        halo_grad[0, c] = own_rows(c, x_hi, got_grad, c)[:, :128].astype(bf)
        halo_grad[1, c] = own_rows(c, x_hi, got_grad, c)[:, 640:].astype(bf)
    grad_copies = fan_out(33, far_grad, far_got_grad, halo_grad, halo_got_grad)

    reduce_y(1)
    reduce_z(0)
    reduce_z(1)
    for copy in grad_copies:
        copy.wait_recv()
    for c in range(2):
        kept = own_rows(c, x_hi, got_grad, c)
        object_out[c] = obj[c] + merged(kept, far_got_grad, halo_got_grad, c) / weight

    final = rims[x_hi, pl.ds(pl.multiple_of(16 * (x % 2), 16), 16)]
    weight = last_power[x % 2, :4] + probe_reg
    for i in range(1, X):
        make(104 + i, rims.at[0, pl.ds(0, 16)], got_x.at[i], sibling).wait_recv()
        final = final + got_x[i]
        power_x(i).wait_recv()
        weight = weight + got_power_x[i, :4]
    at = pl.multiple_of((tile // 2) * 8, 8)
    for k in range(4):
        rows8 = probe[k // 2, k % 2, pl.ds(at, 8), :]
        probe_row = jnp.where(tile % 2 == 0, rows8[:4], rows8[4:])
        probe_out[k] = probe_row + final[4 * k:4 * k + 4] / weight
    for copy in [far, cut, near, own, far_on] + around + planes_on:
        copy.wait_send()
    for flag, copy in zip(sends, halo):
        pl.when(flag)(copy.wait_send)
    for flag, copy in halo_kept:
        pl.when(flag)(copy.wait_send)
    for copy in [power_copy, light_copy, grad_copy, ] + light_copies + grad_copies:
        copy.wait_send()
    for i in range(4):
        passed(i).wait_send()
        for j in range(1, Y):
            to_y(i, j).wait_send()
    for h in range(2):
        for i in range(1, Z):
            to_z(h, i).wait_send()
    for j in range(1, Y):
        power_y(j).wait_send()
    for i in range(1, X):
        make(104 + i, rims.at[0, pl.ds(0, 16)], got_x.at[i], sibling).wait_send()
        power_x(i).wait_send()


def refine(counts, rows, cols, obj, probe, meas):
    whole = pl.BlockSpec(memory_space=pltpu.VMEM)
    scalars = pl.BlockSpec(memory_space=pltpu.SMEM)
    remote = pl.BlockSpec(memory_space=pl.ANY)
    return pl.pallas_call(
        refine_kernel,
        out_shape=(
            jax.ShapeDtypeStruct((2, 128, 512), f32), jax.ShapeDtypeStruct((4, 4, N), f32)
        ),
        in_specs=[scalars] * 3 + [remote] * 4,
        out_specs=(whole, whole),
        scratch_shapes=[
            pltpu.VMEM((2, 128, 512), f32),
            pltpu.VMEM((2, 2, N, N), f32),
            pltpu.VMEM((3, N, N), f32),
            pltpu.VMEM((8, N, N), bf),
            pltpu.VMEM((2, 128, 512), bf),
            pltpu.VMEM((2, 512, 768), bf),
            pltpu.VMEM((4, 4, N, N), bf),
            pltpu.VMEM((3, N, N), f32),
            pltpu.VMEM((3, 768, N), bf),
            pltpu.VMEM((3, N, 512), bf),
            pltpu.VMEM((3, 512, N), bf),
            pltpu.VMEM((3, 2, 512, N), bf),
            pltpu.VMEM((2, N, 3 * N), f32),
            pltpu.VMEM((128, 768), f32),
            pltpu.VMEM((3, 2, N, N), f32),
            pltpu.VMEM((3, N, N), f32),
            pltpu.VMEM((8, 2 * N, 3 * N), f32),
            pltpu.VMEM((N, N), f32),
            pltpu.VMEM((3, N, N), bf),
            pltpu.VMEM((3 * N, 768), bf),
            pltpu.VMEM((2, 512, 768), f32),
            pltpu.VMEM((3, 2, N, N), f32),
            pltpu.VMEM((4, 2, N, N), bf),
            pltpu.VMEM((4, 2, N, N), bf),
            pltpu.VMEM((N, N), bf),
            pltpu.VMEM((N, N), bf),
            pltpu.VMEM((4, 2, 2, Y, 32, N), bf),
            pltpu.VMEM((12, 2, 2, 32, N), bf),
            pltpu.VMEM((2, Y, 32, N), bf),
            pltpu.VMEM((3, 2, 32, N), bf),
            pltpu.VMEM((Z, 48, N), f32),
            pltpu.VMEM((2, Z, 48, N), bf),
            pltpu.VMEM((2, Z, 48, N), bf),
            pltpu.VMEM((2, 32, N), f32),
            pltpu.VMEM((X, 16, N), f32),
            pltpu.VMEM((2, 8, N), f32),
            pltpu.VMEM((X, 8, N), f32),
            pltpu.VMEM((2, 1, 128, 768), bf),
            pltpu.VMEM((2, 1, 128, 768), bf),
            pltpu.VMEM((1, 128, 768), bf),
            pltpu.VMEM((1, 128, 512), bf),
            pltpu.VMEM((2, 1, 128, 128), bf),
            pltpu.VMEM((4, 1, 128, 128), bf),
            pltpu.VMEM((2, 2, 128, 768), bf),
            pltpu.VMEM((2, 2, 128, 768), bf),
            pltpu.VMEM((2, 128, 768), bf),
            pltpu.VMEM((2, 128, 512), bf),
            pltpu.VMEM((2, 2, 128, 128), bf),
            pltpu.VMEM((4, 2, 128, 128), bf),
            pltpu.SemaphoreType.DMA((112,)), pltpu.SemaphoreType.DMA((112,)),
            pltpu.SemaphoreType.DMA((4,)),
        ],
        compiler_params=pltpu.CompilerParams(
            collective_id=1, has_side_effects=True, vmem_limit_bytes=60 * 2**20
        ),
        name="refine",
    )(counts, rows, cols, obj, probe, meas, jnp.asarray(tables()))


def local(object_field, probe, measured, scan_rows, scan_cols, counts):
    object_out, probe_out = refine(counts, scan_rows, scan_cols, object_field, probe, measured)
    return object_out, probe_out.reshape(2, 2, 4, N)


def solution(mesh):
    return jax.shard_map(
        local,
        mesh=mesh,
        in_specs=(
            P(None, "mode", "tile"),
            P("mode", None, None, None),
            P(("tile", "mode"), None, None),
            P(("tile", "mode")),
            P(("tile", "mode")),
            P("tile"),
        ),
        out_specs=(P(None, "mode", "tile"), P("mode", None, "tile", None)),
        check_vma=False,
    )
```

```python
import functools

import jax
import jax.numpy as jnp
import ml_dtypes
import numpy as np
from jax import lax
from jax.experimental import pallas as pl
from jax.experimental.pallas import tpu as pltpu
from jax.sharding import PartitionSpec as P

object_reg = 0.5
probe_reg = 1.0
N = 256
H = N // 2
X, Y, Z = 4, 4, 8
bf = jnp.bfloat16
f32 = jnp.float32
MESH = pl.DeviceIdType.MESH


def tables():
    pos = np.arange(N)
    ang = (pos[:, None] * pos[None, :] % N) * (2.0 * np.pi / N)
    sc = 1.0 / np.sqrt(float(N))
    re = (np.cos(ang) * sc).astype(ml_dtypes.bfloat16)
    im = (-np.sin(ang) * sc).astype(ml_dtypes.bfloat16)
    out = []
    for p in range(2):
        c, s = re[:H, p::2], im[:H, p::2]
        out.append(np.block([[c, s], [-s, c]]))
    for p in range(2):
        c, s = re[p::2, :H], im[p::2, :H]
        out.append(np.block([[c, -s], [s, c]]))
    for p in range(2):
        c, s = re[:H, p::2], im[:H, p::2]
        out.append(np.block([[c, s], [-s, c]]))
    for p in range(2):
        c, s = re[p::2, :H], im[p::2, :H]
        out.append(np.block([[c, -s], [s, c]]))
    return np.stack(out).astype(ml_dtypes.bfloat16)


def side(parts):
    return jnp.concatenate(parts, 1)


def stack(parts):
    return jnp.concatenate(parts, 0)


def dot(a, b):
    return jnp.dot(a, b, preferred_element_type=f32)


def here():
    tile = lax.axis_index("tile")
    group = lax.axis_index("mode")
    x = (group // 2) * 2 + tile // (Y * Z)
    return tile, group, x, (tile // Z) % Y, tile % Z, group % 2


def device(x, y, z, core):
    return {"tile": (x % 2) * (Y * Z) + y * Z + z, "mode": (x // 2) * 2 + core}


def sender(send_sem, recv_sem):
    def make(index, src, dst, target):
        return pltpu.make_async_remote_copy(
            src_ref=src, dst_ref=dst, send_sem=send_sem.at[index], recv_sem=recv_sem.at[index],
            device_id=target, device_id_type=MESH,
        )
    return make


def refine_kernel(counts, rows_in, cols, obj_in, probe_in, meas_in, dft_in, object_out, probe_out,
                  obj, probe, meas, dft, block, ext, modes, powers,
                  from_cols, from_rows, to_rows, narrow, by, kept_light,
                  patch, factor, spec, light, terms, to_cols, total, grads,
                  out_probe, got_probe, out_power, got_power, pieces, got_y, whole_power, got_power_y,
                  wide, bands, got_z, rims, got_x, last_power, got_power_x,
                  out_light, got_light, far_light, far_got_light, halo_light, halo_got_light,
                  out_grad, got_grad, far_grad, far_got_grad, halo_grad, halo_got_grad,
                  send_sem, recv_sem, load_sem):
    loads = [
        pltpu.make_async_copy(src, dst, load_sem.at[i])
        for i, (src, dst) in enumerate(
            ((obj_in, obj), (probe_in, probe), (meas_in, meas), (dft_in, dft))
        )
    ]
    for load in loads:
        load.start()
    slots = 3
    tile, group, x, y, z, core = here()
    tiles = X * Y * Z // 2
    x_hi = group // 2
    sibling = device(x, y, z, 1 - core)
    opposite = device((x + 2) % X, y, z, core)
    before, after = (tile + tiles - 1) % tiles, (tile + 1) % tiles
    other = (group + 2) % 4
    halo_to = [
        {"tile": before, "mode": group}, {"tile": before, "mode": other},
        {"tile": after, "mode": group}, {"tile": after, "mode": other},
    ]
    along_x = [device((x + i) % X, y, z, core) for i in (1, 3, 2)]
    along_z = [device(x, y, (z + i) % Z, core) for i in range(1, Z)]
    make = sender(send_sem, recv_sem)

    across = device(X - 1 - x, y, z, core)
    along_y = [device(x, (y + i) % Y, z, core) for i in (2, 1, 3)]
    partners = [sibling] + halo_to + along_x + along_y + along_z
    barrier = pltpu.get_barrier_semaphore()
    for partner in partners:
        pl.semaphore_signal(barrier, inc=1, device_id=partner, device_id_type=MESH)
    rows = [jnp.where(group * slots + s < counts[0], rows_in[s], 4096) for s in range(slots)]

    mine = pl.multiple_of(group * 128, 128)
    theirs = pl.multiple_of(other * 128, 128)
    loads[0].wait()
    block[...] = obj[...].astype(bf)
    ext[:, pl.ds(mine, 128), 128:640] = block[...]

    @pl.when(tile == 0)
    def _():
        ext[:, :, :128] = jnp.zeros((2, 512, 128), bf)

    @pl.when(tile == tiles - 1)
    def _():
        ext[:, :, 640:] = jnp.zeros((2, 512, 128), bf)

    loads[1].wait()
    for k in range(2):
        for c in range(2):
            modes[group, 2 * k + c] = probe[k, c].astype(bf)
    pl.semaphore_wait(barrier, len(partners))

    def strip(start, low, width):
        return ext.at[:, pl.ds(start, 128), pl.ds(low, width)]

    def plane(which, index):
        return modes.at[which, pl.ds(index, 1)]

    cut = make(41, plane(group, y), plane(group, y), across)
    cut.start()
    own = make(47, modes.at[group], modes.at[group], sibling)
    own.start()
    far = make(40, block, strip(mine, 128, 512), opposite)
    far.start()
    left, right = block.at[:, :, pl.ds(0, 128)], block.at[:, :, pl.ds(384, 128)]
    halo = [
        make(42, left, strip(mine, 640, 128), halo_to[0]),
        make(43, left, strip(mine, 640, 128), halo_to[1]),
        make(44, right, strip(mine, 0, 128), halo_to[2]),
        make(45, right, strip(mine, 0, 128), halo_to[3]),
    ]
    sends = (tile > 0, tile > 0, tile < tiles - 1, tile < tiles - 1)
    gets = (tile < tiles - 1, tile < tiles - 1, tile > 0, tile > 0)
    for i in (1, 3, 0, 2):
        pl.when(sends[i])(halo[i].start)
    near = make(46, block, strip(mine, 128, 512), sibling)
    near.start()

    def pass_on(index, ref):
        copy = make(index, ref, ref, sibling)
        copy.start()
        return copy

    def picks(height, width, shift, down):
        high = lax.broadcasted_iota(jnp.int32, (height, width), 0)
        wide = lax.broadcasted_iota(jnp.int32, (height, width), 1)
        hit = high == wide + shift if down else wide == high + shift
        return jnp.where(hit, 1.0, 0.0).astype(bf)

    def sorted_by_parity(down):
        high = lax.broadcasted_iota(jnp.int32, (N, N), 0)
        wide = lax.broadcasted_iota(jnp.int32, (N, N), 1)
        place, held = (high, wide) if down else (wide, high)
        hit = held == jnp.where(place < N // 2, 2 * place, 2 * place - (N - 1))
        return jnp.where(hit, 1.0, 0.0).astype(f32)

    for s in range(slots):
        from_cols[s] = picks(768, N, cols[s], True)
        from_rows[s] = picks(N, 512, rows[s], False)
        to_rows[s] = picks(512, N, rows[s], True)
        to_cols[s * N:(s + 1) * N, :] = picks(N, 768, cols[s], False)
    light[...] = jnp.zeros_like(light)
    wide[...] = jnp.zeros_like(wide)
    powers[...] = jnp.zeros_like(powers)
    grads[...] = jnp.zeros_like(grads)
    loads[2].wait()
    for s in range(slots):
        by_cols = jnp.dot(meas[s], sorted_by_parity(False), precision=lax.Precision.HIGHEST,
                          preferred_element_type=f32)
        meas[s] = jnp.dot(sorted_by_parity(True), by_cols, precision=lax.Precision.HIGHEST,
                          preferred_element_type=f32)

    def scatter(c):
        spread_rows = [dot(to_rows[s], terms[s]).astype(bf) for s in range(slots)]
        total[c] = dot(jnp.concatenate(spread_rows, 1), to_cols[...])

    def sibling_rows(c, out, k):
        for h in range(2):
            start = pl.multiple_of((2 * h + 1 - core) * 128, 128)
            out[h, k] = total[c, pl.ds(start, 128), :].astype(bf)

    def own_rows(c, h, got, k):
        start = pl.multiple_of((2 * h + core) * 128, 128)
        return total[c, pl.ds(start, 128), :] + got[h, k].astype(f32)

    def fan_out(first, far, far_got, halo, halo_got):
        copies = [
            make(first, far.at[:, :, pl.ds(128, 512)], far_got, opposite),
            make(first + 1, halo.at[0], halo_got.at[0], halo_to[0]),
            make(first + 2, far.at[:, :, pl.ds(0, 128)], halo_got.at[1], halo_to[1]),
            make(first + 3, halo.at[1], halo_got.at[2], halo_to[2]),
            make(first + 4, far.at[:, :, pl.ds(640, 128)], halo_got.at[3], halo_to[3]),
        ]
        for i in (2, 4, 0, 1, 3):
            copies[i].start()
        return copies

    keep_left = jnp.where(tile > 0, 1.0, 0.0)
    keep_right = jnp.where(tile < tiles - 1, 1.0, 0.0)

    def merged(kept, far_got, halo_got, k):
        center = kept[:, 128:640] + far_got[k].astype(f32)
        from_right = (halo_got[0, k].astype(f32) + halo_got[1, k].astype(f32)) * keep_right
        from_left = (halo_got[2, k].astype(f32) + halo_got[3, k].astype(f32)) * keep_left
        return jnp.concatenate(
            [center[:, :128] + from_left, center[:, 128:384], center[:, 384:] + from_right], 1
        )

    cut.wait_recv()
    around = []
    for i, target in enumerate(along_y):
        copy = make(48 + i, plane(other, y), plane(other, y), target)
        copy.start()
        around.append(copy)
    planes_on = [pass_on(51, plane(other, y))]

    def narrow_rows(which):
        start = pl.multiple_of(which * 128, 128)
        for s in range(slots):
            for c in range(2):
                narrow[s, c, pl.ds(start, 128), :] = dot(
                    ext[c, pl.ds(start, 128), :], from_cols[s]
                ).astype(bf)

    halo_kept = []
    for i, (flag, start, low) in enumerate(
        zip(gets, (mine, theirs, mine, theirs), (640, 640, 0, 0))
    ):
        halo_kept.append((flag, make(52 + i, strip(start, low, 128), strip(start, low, 128), sibling)))

    def halo_on(i):
        flag, on = halo_kept[i]

        @pl.when(flag)
        def _():
            halo[i].wait_recv()
            on.start()

    def halo_in(i):
        flag, on = halo_kept[i]
        pl.when(flag)(on.wait_recv)

    halo_on(0)
    halo_on(2)
    narrow_rows(group)
    near.wait_recv()
    halo_in(0)
    halo_in(2)
    narrow_rows(group + 1 - 2 * core)
    halo_on(1)
    halo_on(3)
    far.wait_recv()
    far_on = pass_on(56, strip(theirs, 128, 512))
    narrow_rows(other)
    far_on.wait_recv()
    halo_in(1)
    halo_in(3)
    narrow_rows((other // 2) * 2 + 1 - core)
    for s in range(slots):
        for c in range(2):
            patch[s, c] = dot(from_rows[s], narrow[s, c])
    factor[0] = patch[0, 0] * patch[0, 0] + patch[0, 1] * patch[0, 1]
    for s in range(1, slots):
        factor[0] += patch[s, 0] * patch[s, 0] + patch[s, 1] * patch[s, 1]
    out_power[...] = factor[0].astype(bf)
    power_copy = make(0, out_power, got_power, sibling)
    power_copy.start()
    loads[3].wait()

    def spectra(q, g):
        m = 2 * g + q
        pr = modes[m // 2, 2 * (m % 2)].astype(f32)
        pi = modes[m // 2, 2 * (m % 2) + 1].astype(f32)
        added, taken = [], []
        for s in range(slots):
            re = pr * patch[s, 0] - pi * patch[s, 1]
            im = pr * patch[s, 1] + pi * patch[s, 0]
            added.append(side([re[:, :H] + re[:, H:], im[:, :H] + im[:, H:]]).astype(bf))
            taken.append(side([re[:, :H] - re[:, H:], im[:, :H] - im[:, H:]]).astype(bf))
        even = dot(stack(added), dft[0])
        odd = dot(stack(taken), dft[1])
        added, taken = [], []
        for s in range(slots):
            low, high = slice(s * N, s * N + H), slice(s * N + H, (s + 1) * N)
            e, o = even[low] + even[high], odd[low] + odd[high]
            added.append(stack([side([e[:, :H], o[:, :H]]), side([e[:, H:], o[:, H:]])]).astype(bf))
            e, o = even[low] - even[high], odd[low] - odd[high]
            taken.append(stack([side([e[:, :H], o[:, :H]]), side([e[:, H:], o[:, H:]])]).astype(bf))
        even = dot(dft[2], side(added))
        odd = dot(dft[3], side(taken))
        spec[m, :N] = even
        spec[m, N:] = odd
        for s in range(slots):
            e, o = even[:, s * N:(s + 1) * N], odd[:, s * N:(s + 1) * N]
            powers[s, :H] += e[:H] * e[:H] + e[H:] * e[H:]
            powers[s, H:] += o[:H] * o[:H] + o[H:] * o[H:]
        return g

    def mode_light(g):
        for k in range(2):
            re = modes[g, 2 * k].astype(f32)
            im = modes[g, 2 * k + 1].astype(f32)
            light[...] += re * re + im * im

    near_group = group + 1 - 2 * core
    lax.fori_loop(0, 2, spectra, group, unroll=True)
    for i, step in enumerate((2, 1, 3)):
        around[i].wait_recv()
        planes_on.append(pass_on(57 + i, plane(other, (y + Y - step) % Y)))
    own.wait_recv()
    lax.fori_loop(0, 2, spectra, near_group, unroll=True)
    mode_light(group)
    mode_light(near_group)
    for copy in planes_on:
        copy.wait_recv()
    lax.fori_loop(0, 2, spectra, other, unroll=True)
    lax.fori_loop(0, 2, spectra, (near_group + 2) % 4, unroll=True)
    mode_light(other)
    mode_light((near_group + 2) % 4)
    for s in range(slots):
        terms[s] = light[...].astype(bf)
    scatter(0)
    sibling_rows(0, out_light, 0)
    light_copy = make(1, out_light, got_light, sibling)
    light_copy.start()
    for s in range(slots):
        ratio = meas[s] * lax.rsqrt(jnp.maximum(powers[s], 0.25)) - 1.0
        for p in range(2):
            rows_p = ratio[p * H:(p + 1) * H]
            by[p, :, s * N:(s + 1) * N] = stack([rows_p, rows_p])


    def passed(i):
        return make(60 + i, out_probe.at[i], got_probe.at[i], sibling)

    def to_y(i, j):
        k = 3 * i + j - 1
        return make(70 + k, pieces.at[i, :, :, (y + j) % Y], got_y.at[k], device(x, (y + j) % Y, z, core))

    def power_y(j):
        return make(82 + j, whole_power.at[:, (y + j) % Y], got_power_y.at[j - 1],
                    device(x, (y + j) % Y, z, core))

    def to_z(h, i):
        height = 48 if h == 0 else 32
        return make(
            86 + 8 * h + i, bands.at[h, (z + i) % Z, pl.ds(0, height)],
            got_z.at[h, i, pl.ds(0, height)], along_z[i - 1]
        )

    def to_x(h, xl):
        i = (2 * h + xl - x + X) % X
        return make(104 + i, rims.at[h, pl.ds(16 * xl, 16)], got_x.at[i], device(2 * h + xl, y, z, core)), i

    def power_x(i):
        return make(108 + i, last_power.at[(x + i) % 2], got_power_x.at[i], device((x + i) % X, y, z, core))

    def reduce_y(h):
        for p in range(2):
            i = 2 * h + p
            band = pieces[i, :, :, y].astype(f32)
            for j in range(1, Y):
                to_y(i, j).wait_recv()
                band = band + got_y[3 * i + j - 1].astype(f32)
            for part in range(Z):
                for xl in range(2):
                    for c in range(2):
                        at = 16 * xl + 8 * p + 4 * c
                        wide[part, at:at + 4] = band[c, xl, 4 * part:4 * part + 4]
        if h == 0:
            band = whole_power[:, y].astype(f32)
            for j in range(1, Y):
                power_y(j).wait_recv()
                band = band + got_power_y[j - 1].astype(f32)
            for part in range(Z):
                for xl in range(2):
                    wide[part, 32 + 4 * xl:36 + 4 * xl] = band[xl, 4 * part:4 * part + 4]
        bands[h] = wide[...].astype(bf)
        for i in (4, 3, 5, 2, 6, 1, 7):
            to_z(h, i).start()

    def reduce_z(h):
        height = 48 if h == 0 else 32
        total_z = bands[h, z, :height].astype(f32)
        for i in range(1, Z):
            to_z(h, i).wait_recv()
            total_z = total_z + got_z[h, i, :height].astype(f32)
        rims[h] = total_z[:32]
        for xl in range(2):
            copy, i = to_x(h, xl)
            pl.when(i > 0)(copy.start)
        if h == 0:
            for xl in range(2):
                last_power[xl, :4] = total_z[32 + 4 * xl:36 + 4 * xl]
                last_power[xl, 4:] = total_z[36:40]
            for i in range(1, X):
                power_x(i).start()

    def back_step(step, _):
        i = step // 2
        m = 4 * (i // 2) + 2 * jnp.where(step % 2 == 0, 1 - core, core) + i % 2
        pr = modes[m // 2, 2 * (m % 2)].astype(f32)
        pi = modes[m // 2, 2 * (m % 2) + 1].astype(f32)
        even = dot(dft[4], (spec[m, :N] * by[0]).astype(bf))
        odd = dot(dft[5], (spec[m, N:] * by[1]).astype(bf))
        low, high = (even + odd).astype(bf), (even - odd).astype(bf)
        at_even, at_odd = [], []
        for s in range(slots):
            c, d = slice(s * N, s * N + H), slice(s * N + H, (s + 1) * N)
            at_even.append(side([stack([low[:H, c], high[:H, c]]), stack([low[H:, c], high[H:, c]])]))
            at_odd.append(side([stack([low[:H, d], high[:H, d]]), stack([low[H:, d], high[H:, d]])]))
        even = dot(stack(at_even), dft[6])
        odd = dot(stack(at_odd), dft[7])
        low, high = even + odd, even - odd
        sum_re, sum_im = None, None
        for s in range(slots):
            r = slice(s * N, (s + 1) * N)
            br = side([low[r, :H], high[r, :H]])
            bi = side([low[r, H:], high[r, H:]])
            ar = patch[s, 0]
            ai = patch[s, 1]
            re = ar * br + ai * bi
            im = ar * bi - ai * br
            sum_re = re if s == 0 else sum_re + re
            sum_im = im if s == 0 else sum_im + im
            grads[s, 0] += pr * br + pi * bi
            grads[s, 1] += pr * bi - pi * br

        @pl.when(step % 2 == 0)
        def _():
            out_probe[i, 0] = sum_re.astype(bf)
            out_probe[i, 1] = sum_im.astype(bf)
            passed(i).start()

        @pl.when(step % 2 == 1)
        def _():
            passed(i).wait_recv()
            for c, mine_sum in enumerate((sum_re, sum_im)):
                both = (mine_sum + got_probe[i, c].astype(f32)).astype(bf)
                pieces[i, c] = both.reshape(2, Y, 32, N)
            for j in (2, 1, 3):
                to_y(i, j).start()
        return 0

    power_copy.wait_recv()
    whole_power[...] = (out_power[...].astype(f32) + got_power[...].astype(f32)).astype(bf).reshape(2, Y, 32, N)
    for j in range(1, Y):
        power_y(j).start()
    lax.fori_loop(0, 2, back_step, 0)
    light_copy.wait_recv()
    kept = own_rows(0, x_hi, got_light, 0)
    kept_light[...] = kept
    far_light[0] = own_rows(0, 1 - x_hi, got_light, 0).astype(bf)
    halo_light[0, 0] = kept[:, :128].astype(bf)
    halo_light[1, 0] = kept[:, 640:].astype(bf)
    light_copies = fan_out(2, far_light, far_got_light, halo_light, halo_got_light)
    lax.fori_loop(2, 8, back_step, 0)

    for copy in light_copies:
        copy.wait_recv()
    weight = merged(kept_light[...], far_got_light, halo_got_light, 0) + object_reg

    for c in range(2):
        for s in range(slots):
            terms[s] = grads[s, c].astype(bf)
        scatter(c)
    for c in range(2):
        sibling_rows(c, out_grad, c)
    grad_copy = make(32, out_grad, got_grad, sibling)
    grad_copy.start()
    grad_copy.wait_recv()
    for c in range(2):
        far_grad[c] = own_rows(c, 1 - x_hi, got_grad, c).astype(bf)
        halo_grad[0, c] = own_rows(c, x_hi, got_grad, c)[:, :128].astype(bf)
        halo_grad[1, c] = own_rows(c, x_hi, got_grad, c)[:, 640:].astype(bf)
    grad_copies = fan_out(33, far_grad, far_got_grad, halo_grad, halo_got_grad)

    reduce_y(0)
    reduce_y(1)
    reduce_z(0)
    reduce_z(1)
    for copy in grad_copies:
        copy.wait_recv()
    for c in range(2):
        kept = own_rows(c, x_hi, got_grad, c)
        object_out[c] = obj[c] + merged(kept, far_got_grad, halo_got_grad, c) / weight

    final = rims[x_hi, pl.ds(pl.multiple_of(16 * (x % 2), 16), 16)]
    weight = last_power[x % 2, :4] + probe_reg
    for i in range(1, X):
        make(104 + i, rims.at[0, pl.ds(0, 16)], got_x.at[i], sibling).wait_recv()
        final = final + got_x[i]
        power_x(i).wait_recv()
        weight = weight + got_power_x[i, :4]
    at = pl.multiple_of((tile // 2) * 8, 8)
    for k in range(4):
        rows8 = probe[k // 2, k % 2, pl.ds(at, 8), :]
        probe_row = jnp.where(tile % 2 == 0, rows8[:4], rows8[4:])
        probe_out[k] = probe_row + final[4 * k:4 * k + 4] / weight
    for copy in [far, cut, near, own, far_on] + around + planes_on:
        copy.wait_send()
    for flag, copy in zip(sends, halo):
        pl.when(flag)(copy.wait_send)
    for flag, copy in halo_kept:
        pl.when(flag)(copy.wait_send)
    for copy in [power_copy, light_copy, grad_copy, ] + light_copies + grad_copies:
        copy.wait_send()
    for i in range(4):
        passed(i).wait_send()
        for j in range(1, Y):
            to_y(i, j).wait_send()
    for h in range(2):
        for i in range(1, Z):
            to_z(h, i).wait_send()
    for j in range(1, Y):
        power_y(j).wait_send()
    for i in range(1, X):
        make(104 + i, rims.at[0, pl.ds(0, 16)], got_x.at[i], sibling).wait_send()
        power_x(i).wait_send()


def refine(counts, rows, cols, obj, probe, meas):
    whole = pl.BlockSpec(memory_space=pltpu.VMEM)
    scalars = pl.BlockSpec(memory_space=pltpu.SMEM)
    remote = pl.BlockSpec(memory_space=pl.ANY)
    return pl.pallas_call(
        refine_kernel,
        out_shape=(
            jax.ShapeDtypeStruct((2, 128, 512), f32), jax.ShapeDtypeStruct((4, 4, N), f32)
        ),
        in_specs=[scalars] * 3 + [remote] * 4,
        out_specs=(whole, whole),
        scratch_shapes=[
            pltpu.VMEM((2, 128, 512), f32),
            pltpu.VMEM((2, 2, N, N), f32),
            pltpu.VMEM((3, N, N), f32),
            pltpu.VMEM((8, N, N), bf),
            pltpu.VMEM((2, 128, 512), bf),
            pltpu.VMEM((2, 512, 768), bf),
            pltpu.VMEM((4, 4, N, N), bf),
            pltpu.VMEM((3, N, N), f32),
            pltpu.VMEM((3, 768, N), bf),
            pltpu.VMEM((3, N, 512), bf),
            pltpu.VMEM((3, 512, N), bf),
            pltpu.VMEM((3, 2, 512, N), bf),
            pltpu.VMEM((2, N, 3 * N), f32),
            pltpu.VMEM((128, 768), f32),
            pltpu.VMEM((3, 2, N, N), f32),
            pltpu.VMEM((3, N, N), f32),
            pltpu.VMEM((8, 2 * N, 3 * N), f32),
            pltpu.VMEM((N, N), f32),
            pltpu.VMEM((3, N, N), bf),
            pltpu.VMEM((3 * N, 768), bf),
            pltpu.VMEM((2, 512, 768), f32),
            pltpu.VMEM((3, 2, N, N), f32),
            pltpu.VMEM((4, 2, N, N), bf),
            pltpu.VMEM((4, 2, N, N), bf),
            pltpu.VMEM((N, N), bf),
            pltpu.VMEM((N, N), bf),
            pltpu.VMEM((4, 2, 2, Y, 32, N), bf),
            pltpu.VMEM((12, 2, 2, 32, N), bf),
            pltpu.VMEM((2, Y, 32, N), bf),
            pltpu.VMEM((3, 2, 32, N), bf),
            pltpu.VMEM((Z, 48, N), f32),
            pltpu.VMEM((2, Z, 48, N), bf),
            pltpu.VMEM((2, Z, 48, N), bf),
            pltpu.VMEM((2, 32, N), f32),
            pltpu.VMEM((X, 16, N), f32),
            pltpu.VMEM((2, 8, N), f32),
            pltpu.VMEM((X, 8, N), f32),
            pltpu.VMEM((2, 1, 128, 768), bf),
            pltpu.VMEM((2, 1, 128, 768), bf),
            pltpu.VMEM((1, 128, 768), bf),
            pltpu.VMEM((1, 128, 512), bf),
            pltpu.VMEM((2, 1, 128, 128), bf),
            pltpu.VMEM((4, 1, 128, 128), bf),
            pltpu.VMEM((2, 2, 128, 768), bf),
            pltpu.VMEM((2, 2, 128, 768), bf),
            pltpu.VMEM((2, 128, 768), bf),
            pltpu.VMEM((2, 128, 512), bf),
            pltpu.VMEM((2, 2, 128, 128), bf),
            pltpu.VMEM((4, 2, 128, 128), bf),
            pltpu.SemaphoreType.DMA((112,)), pltpu.SemaphoreType.DMA((112,)),
            pltpu.SemaphoreType.DMA((4,)),
        ],
        compiler_params=pltpu.CompilerParams(
            collective_id=1, has_side_effects=True, vmem_limit_bytes=60 * 2**20
        ),
        name="refine",
    )(counts, rows, cols, obj, probe, meas, jnp.asarray(tables()))


def local(object_field, probe, measured, scan_rows, scan_cols, counts):
    object_out, probe_out = refine(counts, scan_rows, scan_cols, object_field, probe, measured)
    return object_out, probe_out.reshape(2, 2, 4, N)


def solution(mesh):
    return jax.shard_map(
        local,
        mesh=mesh,
        in_specs=(
            P(None, "mode", "tile"),
            P("mode", None, None, None),
            P(("tile", "mode"), None, None),
            P(("tile", "mode")),
            P(("tile", "mode")),
            P("tile"),
        ),
        out_specs=(P(None, "mode", "tile"), P("mode", None, "tile", None)),
        check_vma=False,
    )
```
